512 devices in a mesh: grp: 16 (over y, x_hi, core), proto: 32 (over x_lo, z).
Axes of the slice: x: 4 (x_hi: 2, x_lo: 2; x = x_hi * 2 + x_lo), y: 4, z: 16, core: 2. Of those that a mesh axis runs over, the one named last changes fastest.
Arguments:
- teacher_features: bfloat16 [8192, 256], P('grp'), may hold values from -0.65 to 0.65
- student_features: bfloat16 [8192, 256], P('grp'), may hold values from -0.65 to 0.65
- prototypes: bfloat16 [256, 131072], P(None, 'proto'), may hold values from -0.65 to 0.65
Outputs:
- proto_grad: bfloat16 [256, 131072], P('grp', 'proto')
- student_grad: bfloat16 [8192, 256], P('grp')
- mean_loss: float32 [], replicated
The draws below stay inside these ranges and needn't reach their ends.
All inputs are finite; a program needn't handle non-finite values.
Results may differ from the reference program's by a relative error of at most 0.0043.
Values may be sent and summed in bfloat16 or wider, within the bound.
A program may use at most 64 MiB of HBM per device.

```python
import jax
import jax.numpy as jnp
from jax import lax

BOTTLENECK = 256
PROTO_DEV = 4096
ITERS = 3
ROWS = 8192
PROTOS = 131072
N_PROTO = 32


def shared_direction(key):
    return jax.random.truncated_normal(jax.random.fold_in(key, 977), -3.0, 3.0, (BOTTLENECK,), jnp.float32)


def crop_features(key, direction, shown_loading):
    key_random, key_loading = jax.random.split(key, 2)
    location = jnp.arange(ROWS, dtype=jnp.float32) / ROWS
    growth = (0.5 + location)[:, None]
    random_part = jax.random.truncated_normal(key_random, -3.0, 3.0, (ROWS, BOTTLENECK), jnp.float32)
    loading = jax.random.uniform(key_loading, (ROWS, 1), jnp.float32, -shown_loading, shown_loading) * growth
    return ((random_part + loading * direction[None, :]) / 16.0).astype(jnp.bfloat16)


def draw_teacher_features(key, part):
    direction = shared_direction(key)
    key = jax.random.fold_in(key, 11)
    return crop_features(key, direction, 1.5)


def draw_student_features(key, part):
    direction = shared_direction(key)
    key = jax.random.fold_in(key, 12)
    return crop_features(key, direction, 1.5)


def draw_prototypes(key, part):
    direction = shared_direction(key)
    key = jax.random.fold_in(key, 13)
    key_random, key_loading = jax.random.split(key, 2)
    location = jnp.arange(PROTOS, dtype=jnp.float32) / PROTOS
    growth = (0.5 + location)[None, :]
    random_part = jax.random.truncated_normal(key_random, -3.0, 3.0, (BOTTLENECK, PROTOS), jnp.float32)
    loading = jax.random.uniform(key_loading, (1, PROTOS), jnp.float32, -1.5, 1.5) * growth
    return ((random_part + loading * direction[:, None]) / 16.0).astype(jnp.bfloat16)


def setup_inputs(seed: int = 0) -> dict:
    arg_keys = jax.random.split(jax.random.key(seed), 4)
    return {
        "teacher_features": draw_teacher_features(jax.random.fold_in(arg_keys[3], 71), 0),
        "student_features": draw_student_features(jax.random.fold_in(arg_keys[3], 71), 0),
        "prototypes": draw_prototypes(jax.random.fold_in(arg_keys[3], 71), 0),
    }


teacher_temp = 0.07
student_temp = 0.1
epsilon = 1e-06
highest = lax.Precision.HIGHEST

def unit_rows(features):
    float_rows = features.astype(jnp.float32)
    scaling = lax.rsqrt(lax.optimization_barrier(jnp.sum(float_rows * float_rows, axis=1, keepdims=True)) + epsilon)
    return (float_rows * scaling, scaling)

def reference(teacher_features, student_features, prototypes):
    teacher_wide, teacher_scaling = unit_rows(teacher_features)
    teacher_unit = teacher_wide.astype(jnp.bfloat16)
    student_wide, student_scaling = unit_rows(student_features)
    student_unit = student_wide.astype(jnp.bfloat16)
    proto_float = prototypes.astype(jnp.float32)
    proto_scaling = lax.rsqrt(lax.optimization_barrier(jnp.sum(proto_float * proto_float, axis=0, keepdims=True)) + epsilon)
    proto_wide = proto_float * proto_scaling
    proto_unit = proto_wide.astype(jnp.bfloat16)
    unit_blocks = proto_unit.reshape(BOTTLENECK, N_PROTO, PROTO_DEV).transpose(1, 0, 2)
    wide_blocks = proto_wide.reshape(BOTTLENECK, N_PROTO, PROTO_DEV).transpose(1, 0, 2)
    scaling_blocks = proto_scaling.reshape(N_PROTO, 1, PROTO_DEV)

    def teacher_exp(column_block):
        return jnp.exp(jnp.dot(teacher_unit, column_block, preferred_element_type=jnp.float32) / teacher_temp)

    def student_logits(column_block):
        return jnp.dot(student_unit, column_block, preferred_element_type=jnp.float32) / student_temp
    row_scale = jnp.ones((ROWS,), jnp.float32)
    col_scale = jnp.ones((N_PROTO, PROTO_DEV), jnp.float32)
    for iteration in range(ITERS):

        def column_mass(column_block):
            return jnp.dot(row_scale, teacher_exp(column_block), precision=highest)
        col_mass = lax.map(column_mass, unit_blocks)
        col_scale = 1.0 / (PROTOS * col_mass)

        def row_part(running, pieces):
            column_block, col_part = pieces
            return (running + jnp.dot(teacher_exp(column_block), col_part, precision=highest), None)
        row_sums, unused = lax.scan(row_part, jnp.zeros((ROWS,), jnp.float32), (unit_blocks, col_scale))
        row_scale = 1.0 / (ROWS * row_sums)

    def student_part(running, column_block):
        return (running + lax.optimization_barrier(jnp.sum(jnp.exp(student_logits(column_block)), axis=1)), None)
    student_total, unused = lax.scan(student_part, jnp.zeros((ROWS,), jnp.float32), unit_blocks)
    log_total = jnp.log(student_total)[:, None]

    def backward(running, pieces):
        loss_part, unit_part = running
        column_block, block_wide, block_scaling, col_part = pieces
        targets = ROWS * teacher_exp(column_block) * row_scale[:, None] * col_part[None, :]
        log_probs = student_logits(column_block) - log_total
        probabilities = jnp.exp(log_probs)
        loss_part = loss_part - jnp.sum(targets * log_probs)
        dlogits = ((probabilities - targets) / student_temp).astype(jnp.bfloat16)
        unit_part = unit_part + lax.dot_general(dlogits, column_block, (((1,), (1,)), ((), ())), preferred_element_type=jnp.float32)
        proto_term = lax.dot_general(student_unit, dlogits, (((0,), (0,)), ((), ())), preferred_element_type=jnp.float32)
        column_dots = lax.optimization_barrier(jnp.sum(block_wide * proto_term, axis=0, keepdims=True))
        grad_block = ((proto_term - block_wide * column_dots) * block_scaling).astype(jnp.bfloat16)
        return ((loss_part, unit_part), grad_block)
    start_state = (jnp.zeros((), jnp.float32), jnp.zeros((ROWS, BOTTLENECK), jnp.float32))
    final_state, grad_blocks = lax.scan(backward, start_state, (unit_blocks, wide_blocks, scaling_blocks, col_scale))
    loss_total, unit_grad = final_state
    proto_grad = grad_blocks.transpose(1, 0, 2).reshape(BOTTLENECK, PROTOS)
    row_dots = lax.optimization_barrier(jnp.sum(student_wide * unit_grad, axis=1, keepdims=True))
    student_grad = ((unit_grad - student_wide * row_dots) * student_scaling).astype(jnp.bfloat16)
    mean_loss = loss_total / ROWS
    return (proto_grad, student_grad, mean_loss)
```

```python
import functools
import math

import jax
import jax.numpy as jnp
from jax import lax
from jax.experimental import pallas as pl
from jax.experimental.pallas import tpu as pltpu
from jax.sharding import PartitionSpec as P

MESH = pl.DeviceIdType.MESH
F32 = jnp.float32
BF16 = jnp.bfloat16

ITERS = 3
TEACHER_TEMP = 0.07
STUDENT_TEMP = 0.1
EPSILON = 1e-06
LOG2E = math.log2(math.e)

ROWS = 512
COLS = 4096
WIDTH = 256
GRP = 16
RING = 16
ALL_ROWS = ROWS * GRP
ALL_COLS = COLS * 2 * RING
BLOCK = 512
BLOCKS = COLS // BLOCK
TILES = COLS // 128
SHARE = WIDTH // GRP
CHIPS = 8
OWN = ROWS // (2 * RING)


def lane_broadcast(vector):
    parts = []
    for group in range(4):
        parts.append(jnp.broadcast_to(vector[group : group + 1, :], (128, 128)).T)
    return jnp.concatenate(parts, axis=0)


def fold_lanes(partial):
    parts = []
    for group in range(4):
        block = partial[group * 128 : (group + 1) * 128, :].T
        parts.append(jnp.sum(block, axis=0, keepdims=True))
    return jnp.concatenate(parts, axis=0)


def kernel(
    teacher_hbm,
    student_hbm,
    proto_hbm,
    proto_out,
    student_out,
    loss_out,
    teacher_in,
    student_in,
    proto_in,
    student_unit,
    student_turned,
    proto_unit,
    proto_scale,
    exps,
    soft,
    half,
    row_wide,
    col_sums,
    col_send,
    col_recv,
    col_scale,
    row_send,
    row_pair,
    row_recv,
    unit_part,
    unit_send,
    unit_pair,
    unit_share,
    unit_mine,
    unit_recv,
    term,
    core_send,
    core_recv,
    term_mine,
    term_send,
    term_recv,
    dots,
    dot_send,
    dot_recv,
    in_sem,
    col_ss,
    col_rs,
    rowx_ss,
    rowx_rs,
    rowz_ss,
    rowz_rs,
    unitx_ss,
    unitx_rs,
    unitz_ss,
    unitz_rs,
    outz_ss,
    outz_rs,
    outx_ss,
    outx_rs,
    core_ss,
    core_rs,
    term_ss,
    term_rs,
    dot_ss,
    dot_rs,
):
    grp = lax.axis_index("grp")
    proto = lax.axis_index("proto")
    core = lax.rem(grp, 2)
    chip = lax.div(grp, 2)
    x_lo = lax.div(proto, RING)
    z = lax.rem(proto, RING)
    partner_core = (grp + 1 - 2 * core, proto)
    partner_x = (grp, z + (1 - x_lo) * RING)

    def grp_peer(step):
        return lax.rem(grp + step, GRP)

    def z_peer(step):
        return lax.rem(z + step, RING)

    def chip_peer(step):
        return lax.rem(chip + step, CHIPS)

    def remote(src, dst, send, recv, device):
        return pltpu.make_async_remote_copy(
            src_ref=src, dst_ref=dst, send_sem=send, recv_sem=recv, device_id=device, device_id_type=MESH
        )

    barrier = pltpu.get_barrier_semaphore()

    def greet_grp(step, carry):
        pl.semaphore_signal(barrier, inc=1, device_id=(grp_peer(step), proto), device_id_type=MESH)
        return carry

    def greet_z(step, carry):
        pl.semaphore_signal(barrier, inc=1, device_id=(grp, x_lo * RING + z_peer(step)), device_id_type=MESH)
        return carry

    lax.fori_loop(1, RING, greet_z, 0)
    lax.fori_loop(1, GRP, greet_grp, 0)
    pl.semaphore_signal(barrier, inc=1, device_id=partner_x, device_id_type=MESH)

    loads = [
        pltpu.make_async_copy(teacher_hbm, teacher_in, in_sem.at[0]),
        pltpu.make_async_copy(student_hbm, student_in, in_sem.at[1]),
        pltpu.make_async_copy(proto_hbm, proto_in, in_sem.at[2]),
    ]
    for load in loads:
        load.start()

    def unit_rows(features):
        wide = features.astype(F32)
        scaling = lax.rsqrt(jnp.sum(wide * wide, axis=1, keepdims=True) + EPSILON)
        return wide * scaling, scaling

    loads[0].wait()
    loads[1].wait()
    teacher_in[...] = unit_rows(teacher_in[...])[0].astype(BF16)
    student_unit[...] = unit_rows(student_in[...])[0].astype(BF16)
    loads[2].wait()

    def columns(block):
        return pl.ds(pl.multiple_of(block * BLOCK, BLOCK), BLOCK)

    def teacher_block(block, carry):
        cols = columns(block)
        wide = proto_in[:, cols].astype(F32)
        scaling = lax.rsqrt(jnp.sum(wide * wide, axis=0, keepdims=True) + EPSILON)
        proto_scale[:, cols] = scaling
        unit = (wide * scaling).astype(BF16)
        proto_unit[:, cols] = unit
        product = jnp.dot(teacher_in[...], unit, preferred_element_type=F32)
        values = jnp.exp2(product * (LOG2E / TEACHER_TEMP))
        exps[:, cols] = values
        total = jnp.sum(values, axis=0, keepdims=True)
        for tile in range(BLOCK // 128):
            col_sums[pl.ds(block * (BLOCK // 128) + tile, 1), :] = total[:, tile * 128 : (tile + 1) * 128]
        return carry

    lax.fori_loop(0, BLOCKS, teacher_block, 0)

    pl.semaphore_wait(barrier, GRP - 1 + RING - 1 + 1)

    def col_copy(turn, step):
        peer = grp_peer(step)
        return remote(
            col_send.at[turn], col_recv.at[turn, grp], col_ss.at[turn, step], col_rs.at[turn, grp], (peer, proto)
        )

    def col_start(turn):
        col_send[turn] = col_sums[...].astype(BF16)
        col_recv[turn, grp] = col_sums[...].astype(BF16)
        lax.fori_loop(1, GRP, lambda step, carry: (col_copy(turn, step).start(), carry)[1], 0)

    def col_finish(turn):
        def wait(step, carry):
            peer = grp_peer(step)
            remote(
                col_send.at[turn], col_recv.at[turn, peer], col_ss.at[turn, step], col_rs.at[turn, peer], (peer, proto)
            ).wait()
            return carry

        lax.fori_loop(1, GRP, wait, 0)
        total = col_recv[turn, 0].astype(F32)
        for peer in range(1, GRP):
            total = total + col_recv[turn, peer].astype(F32)
        col_scale[...] = 1.0 / (ALL_COLS * total)

    def row_start(turn):
        rows = pl.ds(0, 4 if turn == 1 else 8)
        copy = remote(
            row_send.at[turn, rows], row_pair.at[turn, rows], rowx_ss.at[turn], rowx_rs.at[turn], partner_x
        )
        copy.start()
        return copy

    def row_ring(turn, copy):
        size = 4 if turn == 1 else 8
        rows = pl.ds(0, size)
        copy.wait()
        total = row_send[turn, rows] + row_pair[turn, rows]
        row_send[turn, rows] = total
        row_recv[turn, z, rows] = total

        def send(step, carry):
            peer = z_peer(step)
            remote(
                row_send.at[turn, rows],
                row_recv.at[turn, z, rows],
                rowz_ss.at[turn, step],
                rowz_rs.at[turn, z],
                (grp, x_lo * RING + peer),
            ).start()
            return carry

        lax.fori_loop(1, RING, send, 0)

    def row_finish(turn):
        size = 4 if turn == 1 else 8
        rows = pl.ds(0, size)

        def wait(step, carry):
            peer = z_peer(step)
            remote(
                row_send.at[turn, rows],
                row_recv.at[turn, peer, rows],
                rowz_ss.at[turn, step],
                rowz_rs.at[turn, peer],
                (grp, x_lo * RING + peer),
            ).wait()
            return carry

        lax.fori_loop(1, RING, wait, 0)
        total = row_recv[turn, 0, rows]
        for peer in range(1, RING):
            total = total + row_recv[turn, peer, rows]
        return total

    def row_pass(last):
        def rows_of(block, carry):
            rows = pl.ds(pl.multiple_of(block * 64, 64), 64)
            partial = jnp.zeros((64, 128), F32)
            for tile in range(TILES):
                cols = pl.ds(tile * 128, 128)
                scaled = exps[rows, cols] * col_scale[pl.ds(tile, 1), :]
                if last:
                    exps[rows, cols] = scaled
                    half[rows, cols] = scaled.astype(BF16)
                partial = partial + scaled
            row_wide[rows, :] = partial
            return carry

        lax.fori_loop(0, ROWS // 64, rows_of, 0)
        return fold_lanes(row_wide[...])

    def col_pass():
        def block_of(block, carry):
            cols = columns(block)
            partial = jnp.zeros((8, BLOCK), F32)
            for group in range(ROWS // 8):
                rows = pl.ds(group * 8, 8)
                scale = row_wide[rows, :]
                partial = partial + exps[rows, cols] * jnp.concatenate([scale] * (BLOCK // 128), axis=1)
            total = jnp.sum(partial, axis=0, keepdims=True)
            for tile in range(BLOCK // 128):
                col_sums[pl.ds(block * (BLOCK // 128) + tile, 1), :] = total[:, tile * 128 : (tile + 1) * 128]
            return carry

        lax.fori_loop(0, BLOCKS, block_of, 0)

    def unit_matmul():
        unit_part[...] = lax.dot_general(
            half[...], proto_unit[...], (((1,), (1,)), ((), ())), preferred_element_type=F32
        )

    half_rows = ROWS // 2

    def unit_start(part):
        unit_send[part] = unit_part[pl.ds(pl.multiple_of((1 - x_lo) * half_rows, half_rows), half_rows), :].astype(BF16)
        unit_mine[part] = unit_part[pl.ds(pl.multiple_of(x_lo * half_rows, half_rows), half_rows), :]
        copy = remote(unit_send.at[part], unit_pair.at[part], unitx_ss.at[part], unitx_rs.at[part], partner_x)
        copy.start()
        return copy

    def own_rows(index):
        return pl.ds(pl.multiple_of(index * OWN, OWN), OWN)

    def unit_ring(part, copy):
        copy.wait()
        total = unit_mine[part] + unit_pair[part].astype(F32)
        unit_mine[part] = total
        unit_share[part] = total.astype(BF16)

        def send(step, carry):
            peer = z_peer(step)
            remote(
                unit_share.at[part, own_rows(peer)],
                unit_recv.at[part, z],
                unitz_ss.at[part, step],
                unitz_rs.at[part, z],
                (grp, x_lo * RING + peer),
            ).start()
            return carry

        lax.fori_loop(1, RING, send, 0)

    def unit_finish(part):
        def wait(step, total):
            peer = z_peer(step)
            remote(
                unit_share.at[part, own_rows(peer)],
                unit_recv.at[part, peer],
                unitz_ss.at[part, step],
                unitz_rs.at[part, peer],
                (grp, x_lo * RING + peer),
            ).wait()
            return total + unit_recv[part, peer].astype(F32)

        return lax.fori_loop(1, RING, wait, unit_mine[part, own_rows(z), :])

    col_start(0)

    def student_block(block, carry):
        cols = columns(block)
        product = jnp.dot(student_unit[...], proto_unit[:, cols], preferred_element_type=F32)
        values = jnp.exp2(product * (LOG2E / STUDENT_TEMP))
        soft[:, cols] = values
        partial = values[:, :128]
        for tile in range(1, BLOCK // 128):
            partial = partial + values[:, tile * 128 : (tile + 1) * 128]
        row_wide[...] = row_wide[...] + partial
        return carry

    row_wide[...] = jnp.zeros((ROWS, 128), F32)
    lax.fori_loop(0, BLOCKS, student_block, 0)
    row_send[0, 4:8] = fold_lanes(row_wide[...])
    col_finish(0)
    row_send[0, 0:4] = row_pass(False)
    copy = row_start(0)
    row_ring(0, copy)
    sums = row_finish(0)
    row_scale = 1.0 / (ALL_ROWS * sums[0:4])
    student_total = sums[4:8]

    row_wide[...] = lane_broadcast(row_scale)
    col_pass()
    col_start(1)
    row_wide[...] = lane_broadcast((1.0 / STUDENT_TEMP) / student_total)

    def soft_rows(block, carry):
        rows = pl.ds(pl.multiple_of(block * 64, 64), 64)
        scale = row_wide[rows, :]
        for tile in range(TILES):
            cols = pl.ds(tile * 128, 128)
            scaled = soft[rows, cols] * scale
            soft[rows, cols] = scaled
            half[rows, cols] = scaled.astype(BF16)
        return carry

    lax.fori_loop(0, ROWS // 64, soft_rows, 0)
    unit_matmul()
    unit_copy = unit_start(0)
    col_finish(1)
    row_send[1, 0:4] = row_pass(False)
    copy = row_start(1)
    row_ring(1, copy)
    student_turned[...] = student_unit[...].astype(F32).T.astype(BF16)
    row_scale = 1.0 / (ALL_ROWS * row_finish(1))

    row_wide[...] = lane_broadcast(row_scale)
    col_pass()
    col_start(2)
    unit_ring(0, unit_copy)
    col_finish(2)
    row_send[2, 0:4] = row_pass(True)
    unit_matmul()
    row_wide[...] = unit_part[:, :128] * student_unit[:, :128].astype(F32) + unit_part[:, 128:] * student_unit[
        :, 128:
    ].astype(F32)
    row_send[2, 4:8] = fold_lanes(row_wide[...])
    copy = row_start(2)
    unit_copy = unit_start(1)
    row_ring(2, copy)
    unit_ring(1, unit_copy)
    soft_unit = unit_finish(0)
    sums = row_finish(2)
    row_scale = 1.0 / (ALL_ROWS * sums[0:4])
    agreement = (ALL_ROWS / STUDENT_TEMP) * row_scale * sums[4:8]
    loss_here = jnp.sum(jnp.log(student_total) - agreement) * (1.0 / ALL_ROWS)
    row_wide[...] = lane_broadcast((ALL_ROWS / STUDENT_TEMP) * row_scale)

    def core_copy(block):
        return remote(core_send.at[block], core_recv.at[block], core_ss.at[block], core_rs.at[block], partner_core)

    def term_ring(block):
        core_copy(block).wait()
        total = term_mine[block] + core_recv[block].astype(F32)
        term_mine[block] = total
        term_send[block] = total.astype(BF16)

        def send(step, carry):
            peer = chip_peer(step)
            remote(
                term_send.at[block, peer],
                term_recv.at[block, chip],
                term_ss.at[block, step],
                term_rs.at[block, chip],
                (peer * 2 + core, proto),
            ).start()
            return carry

        lax.fori_loop(1, CHIPS, send, 0)

    def term_block(block, carry):
        cols = columns(block)
        scale = row_wide[...]

        wide_scale = jnp.concatenate([scale] * (BLOCK // 128), axis=1)
        half[:, cols] = (soft[:, cols] - exps[:, cols] * wide_scale).astype(BF16)
        product = jnp.dot(student_turned[...], half[:, cols], preferred_element_type=F32)
        total = jnp.sum(product * proto_in[:, cols].astype(F32), axis=0, keepdims=True) * proto_scale[:, cols]
        for tile in range(BLOCK // 128):
            dots[pl.ds(block * (BLOCK // 128) + tile, 1), :] = total[:, tile * 128 : (tile + 1) * 128]
        term[...] = product.reshape(CHIPS, 2, SHARE, BLOCK)
        core_send[block] = term[:, 1 - core].astype(BF16)
        term_mine[block] = term[:, core]
        core_copy(block).start()

        @pl.when(block > 0)
        def _():
            term_ring(block - 1)

        return carry

    lax.fori_loop(0, BLOCKS, term_block, 0)
    term_ring(BLOCKS - 1)

    high = loss_here.astype(BF16).astype(F32)
    middle = (loss_here - high).astype(BF16).astype(F32)
    low = loss_here - high - middle
    place = lax.broadcasted_iota(jnp.int32, (16, 128), 0)
    pieces = jnp.where(place == 0, high, jnp.where(place == 1, middle, jnp.where(place == 2, low, 0.0)))
    dot_send[0:TILES] = dots[...].astype(BF16)
    dot_send[TILES : TILES + 16] = pieces.astype(BF16)
    dot_recv[grp] = dot_send[...]

    def dot_start(step, carry):
        peer = grp_peer(step)
        remote(dot_send, dot_recv.at[grp], dot_ss.at[step], dot_rs.at[grp], (peer, proto)).start()
        return carry

    lax.fori_loop(1, GRP, dot_start, 0)

    target_unit = unit_finish(1)
    my_rows = own_rows(x_lo * RING + z)
    unit_grad = soft_unit - target_unit * row_wide[my_rows, 0:1]
    wide, scaling = unit_rows(student_in[my_rows, :])
    row_dots = jnp.sum(wide * unit_grad, axis=1, keepdims=True)
    student_out[my_rows, :] = ((unit_grad - wide * row_dots) * scaling).astype(BF16)

    def out_copy(step, owner):
        peer = z_peer(step)
        rows = own_rows(x_lo * RING + owner)
        return remote(
            student_out.at[rows],
            student_out.at[rows],
            outz_ss.at[step],
            outz_rs.at[owner],
            (grp, x_lo * RING + peer),
        )

    lax.fori_loop(1, RING, lambda step, carry: (out_copy(step, z).start(), carry)[1], 0)

    def dot_wait(step, carry):
        peer = grp_peer(step)
        remote(dot_send, dot_recv.at[peer], dot_ss.at[step], dot_rs.at[peer], (peer, proto)).wait()
        return carry

    lax.fori_loop(1, GRP, dot_wait, 0)
    total = dot_recv[0].astype(F32)
    for peer in range(1, GRP):
        total = total + dot_recv[peer].astype(F32)
    dots[...] = total[0:TILES]
    loss_out[...] = total[TILES : TILES + 1] + total[TILES + 1 : TILES + 2] + total[TILES + 2 : TILES + 3]

    def term_finish(block, carry):
        cols = columns(block)

        def wait(step, total):
            peer = chip_peer(step)
            remote(
                term_send.at[block, peer],
                term_recv.at[block, peer],
                term_ss.at[block, step],
                term_rs.at[block, peer],
                (peer * 2 + core, proto),
            ).wait()
            return total + term_recv[block, peer].astype(F32)

        total = lax.fori_loop(1, CHIPS, wait, term_mine[block, chip])
        scaling = proto_scale[:, cols]
        wide = proto_in[pl.ds(pl.multiple_of(grp * SHARE, SHARE), SHARE), cols].astype(F32) * scaling
        dot = jnp.concatenate(
            [dots[pl.ds(block * (BLOCK // 128) + tile, 1), :] for tile in range(BLOCK // 128)], axis=1
        )
        proto_out[:, cols] = ((total - wide * dot) * scaling).astype(BF16)
        return carry

    lax.fori_loop(0, BLOCKS, term_finish, 0)

    def out_wait(step, carry):
        peer = z_peer(step)
        out_copy(step, z).wait_send()
        out_copy(step, peer).wait_recv()
        return carry

    lax.fori_loop(1, RING, out_wait, 0)
    mine = pl.ds(pl.multiple_of(x_lo * half_rows, half_rows), half_rows)
    other = pl.ds(pl.multiple_of((1 - x_lo) * half_rows, half_rows), half_rows)
    remote(student_out.at[mine], student_out.at[mine], outx_ss, outx_rs, partner_x).start()
    remote(student_out.at[mine], student_out.at[mine], outx_ss, outx_rs, partner_x).wait_send()
    remote(student_out.at[other], student_out.at[other], outx_ss, outx_rs, partner_x).wait_recv()


def per_device(teacher_features, student_features, prototypes):
    vmem = pltpu.VMEM
    dma = pltpu.SemaphoreType.DMA
    proto_grad, student_grad, loss = pl.pallas_call(
        kernel,
        out_shape=(
            jax.ShapeDtypeStruct((SHARE, COLS), BF16),
            jax.ShapeDtypeStruct((ROWS, WIDTH), BF16),
            jax.ShapeDtypeStruct((1, 128), F32),
        ),
        in_specs=[pl.BlockSpec(memory_space=pl.ANY)] * 3,
        out_specs=(pl.BlockSpec(memory_space=vmem),) * 3,
        scratch_shapes=[
            vmem((ROWS, WIDTH), BF16),
            vmem((ROWS, WIDTH), BF16),
            vmem((WIDTH, COLS), BF16),
            vmem((ROWS, WIDTH), BF16),
            vmem((WIDTH, ROWS), BF16),
            vmem((WIDTH, COLS), BF16),
            vmem((1, COLS), F32),
            vmem((ROWS, COLS), F32),
            vmem((ROWS, COLS), F32),
            vmem((ROWS, COLS), BF16),
            vmem((ROWS, 128), F32),
            vmem((TILES, 128), F32),
            vmem((ITERS, TILES, 128), BF16),
            vmem((ITERS, GRP, TILES, 128), BF16),
            vmem((TILES, 128), F32),
            vmem((ITERS, 8, 128), F32),
            vmem((ITERS, 8, 128), F32),
            vmem((ITERS, RING, 8, 128), F32),
            vmem((ROWS, WIDTH), F32),
            vmem((2, ROWS // 2, WIDTH), BF16),
            vmem((2, ROWS // 2, WIDTH), BF16),
            vmem((2, ROWS // 2, WIDTH), BF16),
            vmem((2, ROWS // 2, WIDTH), F32),
            vmem((2, RING, OWN, WIDTH), BF16),
            vmem((CHIPS, 2, SHARE, BLOCK), F32),
            vmem((BLOCKS, CHIPS, SHARE, BLOCK), BF16),
            vmem((BLOCKS, CHIPS, SHARE, BLOCK), BF16),
            vmem((BLOCKS, CHIPS, SHARE, BLOCK), F32),
            vmem((BLOCKS, CHIPS, SHARE, BLOCK), BF16),
            vmem((BLOCKS, CHIPS, SHARE, BLOCK), BF16),
            vmem((TILES, 128), F32),
            vmem((TILES + 16, 128), BF16),
            vmem((GRP, TILES + 16, 128), BF16),
            dma((3,)),
            dma((ITERS, GRP)),
            dma((ITERS, GRP)),
            dma((ITERS,)),
            dma((ITERS,)),
            dma((ITERS, RING)),
            dma((ITERS, RING)),
            dma((2,)),
            dma((2,)),
            dma((2, RING)),
            dma((2, RING)),
            dma((RING,)),
            dma((RING,)),
            dma,
            dma,
            dma((BLOCKS,)),
            dma((BLOCKS,)),
            dma((BLOCKS, CHIPS)),
            dma((BLOCKS, CHIPS)),
            dma((GRP,)),
            dma((GRP,)),
        ],
        compiler_params=pltpu.CompilerParams(
            collective_id=0, has_side_effects=True, vmem_limit_bytes=56 * 2**20
        ),
        name="sinkhorn_step",
    )(teacher_features, student_features, prototypes)
    return proto_grad, student_grad, loss[0, 0]


def solution(mesh):
    placed = (P("grp", None), P("grp", None), P(None, "proto"))
    return jax.shard_map(
        per_device,
        mesh=mesh,
        in_specs=placed,
        out_specs=(P("grp", "proto"), P("grp", None), P()),
        check_vma=False,
    )
```

```python
import functools
import math

import jax
import jax.numpy as jnp
from jax import lax
from jax.experimental import pallas as pl
from jax.experimental.pallas import tpu as pltpu
from jax.sharding import PartitionSpec as P

MESH = pl.DeviceIdType.MESH
F32 = jnp.float32
BF16 = jnp.bfloat16

ITERS = 3
TEACHER_TEMP = 0.07
STUDENT_TEMP = 0.1
EPSILON = 1e-06
LOG2E = math.log2(math.e)

ROWS = 512
COLS = 4096
WIDTH = 256
GRP = 16
RING = 16
ALL_ROWS = ROWS * GRP
ALL_COLS = COLS * 2 * RING
BLOCK = 512
BLOCKS = COLS // BLOCK
TILES = COLS // 128
TERM_BLOCK = 1024
TERM_BLOCKS = COLS // TERM_BLOCK
HALF_ROWS = ROWS // 2
SHARE = WIDTH // GRP
CHIPS = 8
OWN = ROWS // (2 * RING)


def lane_broadcast(vector):
    parts = []
    for group in range(4):
        parts.append(jnp.broadcast_to(vector[group : group + 1, :], (128, 128)).T)
    return jnp.concatenate(parts, axis=0)


def fold_lanes(partial):
    parts = []
    for group in range(4):
        block = partial[group * 128 : (group + 1) * 128, :].T
        parts.append(jnp.sum(block, axis=0, keepdims=True))
    return jnp.concatenate(parts, axis=0)


def kernel(
    teacher_hbm,
    student_hbm,
    proto_hbm,
    proto_out,
    student_out,
    loss_out,
    teacher_in,
    student_in,
    proto_in,
    student_unit,
    student_turned,
    proto_unit,
    proto_turned,
    proto_scale,
    exps,
    soft,
    soft_half,
    target_half,
    row_wide,
    col_sums,
    col_send,
    col_recv,
    col_scale,
    row_send,
    row_pair,
    row_recv,
    loss_row,
    loss_pair,
    loss_recv,
    unit_part,
    unit_send,
    unit_pair,
    unit_share,
    unit_mine,
    unit_recv,
    term,
    core_send,
    core_recv,
    term_mine,
    term_send,
    term_recv,
    dots,
    dot_send,
    dot_recv,
    in_sem,
    col_ss,
    col_rs,
    rowx_ss,
    rowx_rs,
    rowz_ss,
    rowz_rs,
    lossx_ss,
    lossx_rs,
    lossz_ss,
    lossz_rs,
    unitx_ss,
    unitx_rs,
    unitz_ss,
    unitz_rs,
    outz_ss,
    outz_rs,
    outx_ss,
    outx_rs,
    core_ss,
    core_rs,
    term_ss,
    term_rs,
    dot_ss,
    dot_rs,
):
    grp = lax.axis_index("grp")
    proto = lax.axis_index("proto")
    core = lax.rem(grp, 2)
    chip = lax.div(grp, 2)
    x_lo = lax.div(proto, RING)
    z = lax.rem(proto, RING)
    partner_core = (grp + 1 - 2 * core, proto)
    partner_x = (grp, z + (1 - x_lo) * RING)

    def grp_peer(step):
        return lax.rem(grp + step, GRP)

    def z_peer(step):
        return lax.rem(z + step, RING)

    def chip_peer(step):
        return lax.rem(chip + step, CHIPS)

    def each_z(visit):
        visit(RING // 2)

        def pair(step, carry):
            visit(RING // 2 - step)
            visit(RING // 2 + step)
            return carry

        lax.fori_loop(1, RING // 2, pair, 0)

    def remote(src, dst, send, recv, device):
        return pltpu.make_async_remote_copy(
            src_ref=src, dst_ref=dst, send_sem=send, recv_sem=recv, device_id=device, device_id_type=MESH
        )

    barrier = pltpu.get_barrier_semaphore()

    def greet_grp(step, carry):
        pl.semaphore_signal(barrier, inc=1, device_id=(grp_peer(step), proto), device_id_type=MESH)
        return carry

    def greet_z(step, carry):
        pl.semaphore_signal(barrier, inc=1, device_id=(grp, x_lo * RING + z_peer(step)), device_id_type=MESH)
        return carry

    lax.fori_loop(1, RING, greet_z, 0)
    lax.fori_loop(1, GRP, greet_grp, 0)
    pl.semaphore_signal(barrier, inc=1, device_id=partner_x, device_id_type=MESH)

    loads = [
        pltpu.make_async_copy(teacher_hbm, teacher_in, in_sem.at[0]),
        pltpu.make_async_copy(student_hbm, student_in, in_sem.at[1]),
    ]

    def columns(block, size=BLOCK):
        return pl.ds(pl.multiple_of(block * size, size), size)

    def proto_load(block):
        cols = columns(block)
        return pltpu.make_async_copy(proto_hbm.at[:, cols], proto_in.at[:, cols], in_sem.at[2 + block])

    loads[0].start()
    lax.fori_loop(0, BLOCKS, lambda block, carry: (proto_load(block).start(), carry)[1], 0)
    loads[1].start()

    def unit_rows(features):
        wide = features.astype(F32)
        scaling = lax.rsqrt(jnp.sum(wide * wide, axis=1, keepdims=True) + EPSILON)
        return wide * scaling, scaling

    loads[0].wait()
    teacher_in[...] = unit_rows(teacher_in[...])[0].astype(BF16)

    def teacher_block(block, carry):
        proto_load(block).wait()
        cols = columns(block)
        wide = proto_in[:, cols].astype(F32)
        scaling = lax.rsqrt(jnp.sum(wide * wide, axis=0, keepdims=True) + EPSILON)
        proto_scale[:, cols] = scaling
        unit = (wide * scaling).astype(BF16)
        proto_unit[:, cols] = unit
        product = jnp.dot(teacher_in[...], unit, preferred_element_type=F32)
        values = jnp.exp2(product * (LOG2E / TEACHER_TEMP))
        exps[:, cols] = values
        total = jnp.sum(values, axis=0, keepdims=True)
        for tile in range(BLOCK // 128):
            col_sums[pl.ds(block * (BLOCK // 128) + tile, 1), :] = total[:, tile * 128 : (tile + 1) * 128]
        return carry

    lax.fori_loop(0, BLOCKS, teacher_block, 0)

    pl.semaphore_wait(barrier, GRP - 1 + RING - 1 + 1)

    def col_copy(turn, step):
        peer = grp_peer(step)
        return remote(
            col_send.at[turn], col_recv.at[turn, grp], col_ss.at[turn, step], col_rs.at[turn, grp], (peer, proto)
        )

    def col_start(turn):
        col_send[turn] = col_sums[...].astype(BF16)
        col_recv[turn, grp] = col_sums[...].astype(BF16)
        lax.fori_loop(1, GRP, lambda step, carry: (col_copy(turn, step).start(), carry)[1], 0)

    def col_finish(turn):
        def wait(step, carry):
            peer = grp_peer(step)
            remote(
                col_send.at[turn], col_recv.at[turn, peer], col_ss.at[turn, step], col_rs.at[turn, peer], (peer, proto)
            ).wait()
            return carry

        lax.fori_loop(1, GRP, wait, 0)
        total = col_recv[turn, 0].astype(F32)
        for peer in range(1, GRP):
            total = total + col_recv[turn, peer].astype(F32)
        col_scale[...] = 1.0 / (ALL_COLS * total)

    def pair_copy(send, pair, send_sem, recv_sem):
        return remote(send, pair, send_sem, recv_sem, partner_x)

    def ring_start(source, slots, send_sems, recv_sems):
        def send(step):
            peer = z_peer(step)
            remote(
                source, slots.at[z], send_sems.at[step], recv_sems.at[z], (grp, x_lo * RING + peer)
            ).start()

        each_z(send)

    def ring_sum(source, slots, send_sems, recv_sems):
        def wait(step, carry):
            peer = z_peer(step)
            remote(
                source, slots.at[peer], send_sems.at[step], recv_sems.at[peer], (grp, x_lo * RING + peer)
            ).wait()
            return carry

        lax.fori_loop(1, RING, wait, 0)
        total = slots[0]
        for peer in range(1, RING):
            total = total + slots[peer]
        return total

    def row_refs(turn):
        rows = pl.ds(0, 8 if turn == 0 else 4)
        return row_send.at[turn, rows], row_pair.at[turn, rows], row_recv.at[turn, :, rows]

    def row_start(turn):
        send, pair, slots = row_refs(turn)
        copy = pair_copy(send, pair, rowx_ss.at[turn], rowx_rs.at[turn])
        copy.start()
        return copy

    def row_ring(turn, copy):
        send, pair, slots = row_refs(turn)
        copy.wait()
        total = send[...] + pair[...]
        send[...] = total
        slots[z] = total
        ring_start(send, slots, rowz_ss.at[turn], rowz_rs.at[turn])

    def row_finish(turn):
        send, pair, slots = row_refs(turn)
        return ring_sum(send, slots, rowz_ss.at[turn], rowz_rs.at[turn])

    def row_pass():
        def rows_of(block, carry):
            rows = pl.ds(pl.multiple_of(block * 64, 64), 64)
            partial = jnp.zeros((64, 128), F32)
            for tile in range(TILES):
                partial = partial + exps[rows, pl.ds(tile * 128, 128)] * col_scale[pl.ds(tile, 1), :]
            row_wide[rows, :] = partial
            return carry

        lax.fori_loop(0, ROWS // 64, rows_of, 0)
        return fold_lanes(row_wide[...])

    def target_pass():
        def rows_of(block, carry):
            rows = pl.ds(pl.multiple_of(block * 64, 64), 64)
            partial = jnp.zeros((64, 128), F32)
            for tile in range(TILES):
                cols = pl.ds(tile * 128, 128)
                scaled = exps[rows, cols] * col_scale[pl.ds(tile, 1), :]
                target_half[rows, cols] = scaled.astype(BF16)
                partial = partial + scaled
            row_wide[rows, :] = partial
            return carry

        lax.fori_loop(0, ROWS // 64, rows_of, 0)
        return fold_lanes(row_wide[...])

    def col_pass():
        def block_of(block, carry):
            cols = columns(block)
            partial = jnp.zeros((8, BLOCK), F32)
            for group in range(ROWS // 8):
                rows = pl.ds(group * 8, 8)
                scale = row_wide[rows, :]
                partial = partial + exps[rows, cols] * jnp.concatenate([scale] * (BLOCK // 128), axis=1)
            total = jnp.sum(partial, axis=0, keepdims=True)
            for tile in range(BLOCK // 128):
                col_sums[pl.ds(block * (BLOCK // 128) + tile, 1), :] = total[:, tile * 128 : (tile + 1) * 128]
            return carry

        lax.fori_loop(0, BLOCKS, block_of, 0)

    mine = pl.ds(pl.multiple_of(x_lo * HALF_ROWS, HALF_ROWS), HALF_ROWS)
    other = pl.ds(pl.multiple_of((1 - x_lo) * HALF_ROWS, HALF_ROWS), HALF_ROWS)

    def unit_matmul(source, rows):
        unit_part[rows, :] = jnp.dot(source[rows, :], proto_turned[...], preferred_element_type=F32)

    def unit_start(part):
        unit_send[part] = unit_part[other, :].astype(BF16)
        copy = pair_copy(unit_send.at[part], unit_pair.at[part], unitx_ss.at[part], unitx_rs.at[part])
        copy.start()
        return copy

    def own_rows(index):
        return pl.ds(pl.multiple_of(index * OWN, OWN), OWN)

    def unit_ring(part, copy):
        copy.wait()
        total = unit_part[mine, :] + unit_pair[part].astype(F32)
        unit_mine[part] = total
        unit_share[part] = total.astype(BF16)

        def send(step):
            peer = z_peer(step)
            remote(
                unit_share.at[part, own_rows(peer)],
                unit_recv.at[part, z],
                unitz_ss.at[part, step],
                unitz_rs.at[part, z],
                (grp, x_lo * RING + peer),
            ).start()

        each_z(send)

    def unit_finish(part):
        def wait(step, total):
            peer = z_peer(step)
            remote(
                unit_share.at[part, own_rows(peer)],
                unit_recv.at[part, peer],
                unitz_ss.at[part, step],
                unitz_rs.at[part, peer],
                (grp, x_lo * RING + peer),
            ).wait()
            return total + unit_recv[part, peer].astype(F32)

        return lax.fori_loop(1, RING, wait, unit_mine[part, own_rows(z), :])

    col_start(0)
    loads[1].wait()
    student_unit[...] = unit_rows(student_in[...])[0].astype(BF16)

    def student_block(block, carry):
        cols = columns(block)
        product = jnp.dot(student_unit[...], proto_unit[:, cols], preferred_element_type=F32)
        values = jnp.exp2(product * (LOG2E / STUDENT_TEMP))
        soft[:, cols] = values
        partial = values[:, :128]
        for tile in range(1, BLOCK // 128):
            partial = partial + values[:, tile * 128 : (tile + 1) * 128]
        row_wide[...] = row_wide[...] + partial
        return carry

    row_wide[...] = jnp.zeros((ROWS, 128), F32)
    lax.fori_loop(0, BLOCKS, student_block, 0)
    row_send[0, 4:8] = fold_lanes(row_wide[...])
    col_finish(0)
    row_send[0, 0:4] = row_pass()
    copy = row_start(0)
    student_turned[...] = student_unit[...].astype(F32).T.astype(BF16)
    row_ring(0, copy)

    def turn_block(block, carry):
        cols = columns(block)
        proto_turned[cols, :] = proto_unit[:, cols].T
        return carry

    lax.fori_loop(0, BLOCKS, turn_block, 0)
    sums = row_finish(0)
    row_scale = 1.0 / (ALL_ROWS * sums[0:4])
    student_total = sums[4:8]

    row_wide[...] = lane_broadcast(row_scale)
    col_pass()
    col_start(1)
    row_wide[...] = lane_broadcast((1.0 / STUDENT_TEMP) / student_total)

    def soft_rows(block, carry):
        rows = pl.ds(pl.multiple_of(block * 64, 64), 64)
        scale = row_wide[rows, :]
        for tile in range(TILES):
            cols = pl.ds(tile * 128, 128)
            soft_half[rows, cols] = (soft[rows, cols] * scale).astype(BF16)
        return carry

    lax.fori_loop(0, ROWS // 64, soft_rows, 0)
    unit_matmul(soft_half, pl.ds(0, ROWS))
    col_finish(1)
    row_send[1, 0:4] = row_pass()
    copy = row_start(1)
    row_ring(1, copy)
    unit_copy = unit_start(0)
    row_scale = 1.0 / (ALL_ROWS * row_finish(1))

    row_wide[...] = lane_broadcast(row_scale)
    col_pass()
    col_start(2)
    unit_ring(0, unit_copy)
    col_finish(2)
    row_send[2, 0:4] = target_pass()
    copy = row_start(2)
    unit_matmul(target_half, other)
    unit_copy = unit_start(1)
    unit_matmul(target_half, mine)
    row_ring(2, copy)
    row_wide[...] = unit_part[:, :128] * student_unit[:, :128].astype(F32) + unit_part[:, 128:] * student_unit[
        :, 128:
    ].astype(F32)
    loss_row[...] = fold_lanes(row_wide[...])
    loss_copy = pair_copy(loss_row, loss_pair, lossx_ss, lossx_rs)
    loss_copy.start()
    unit_ring(1, unit_copy)
    loss_copy.wait()
    loss_row[...] = loss_row[...] + loss_pair[...]
    loss_recv[z] = loss_row[...]
    ring_start(loss_row, loss_recv, lossz_ss, lossz_rs)
    soft_unit = unit_finish(0)
    row_scale = 1.0 / (ALL_ROWS * row_finish(2))
    row_wide[...] = lane_broadcast((ALL_ROWS / STUDENT_TEMP) * row_scale)

    def core_copy(block):
        return remote(core_send.at[block], core_recv.at[block], core_ss.at[block], core_rs.at[block], partner_core)

    def term_ring(block):
        core_copy(block).wait()
        total = term_mine[block] + core_recv[block].astype(F32)
        term_mine[block] = total
        term_send[block] = total.astype(BF16)

        def send(step, carry):
            peer = chip_peer(step)
            remote(
                term_send.at[block, peer],
                term_recv.at[block, chip],
                term_ss.at[block, step],
                term_rs.at[block, chip],
                (peer * 2 + core, proto),
            ).start()
            return carry

        lax.fori_loop(1, CHIPS, send, 0)

    def term_block(block, carry):
        cols = columns(block, TERM_BLOCK)
        scale = jnp.concatenate([row_wide[...]] * (TERM_BLOCK // 128), axis=1)
        dlogits = (soft_half[:, cols].astype(F32) - target_half[:, cols].astype(F32) * scale).astype(BF16)
        product = jnp.dot(student_turned[...], dlogits, preferred_element_type=F32)
        term[...] = product.reshape(CHIPS, 2, SHARE, TERM_BLOCK)
        core_send[block] = term[:, 1 - core].astype(BF16)
        core_copy(block).start()
        term_mine[block] = term[:, core]
        total = jnp.sum(product * proto_in[:, cols].astype(F32), axis=0, keepdims=True) * proto_scale[:, cols]
        for tile in range(TERM_BLOCK // 128):
            dots[pl.ds(block * (TERM_BLOCK // 128) + tile, 1), :] = total[:, tile * 128 : (tile + 1) * 128]

        @pl.when(block > 0)
        def _():
            term_ring(block - 1)

        return carry

    lax.fori_loop(0, TERM_BLOCKS, term_block, 0)
    term_ring(TERM_BLOCKS - 1)
    agreement = (ALL_ROWS / STUDENT_TEMP) * row_scale * ring_sum(loss_row, loss_recv, lossz_ss, lossz_rs)
    loss_here = jnp.sum(jnp.log(student_total) - agreement) * (1.0 / ALL_ROWS)

    high = loss_here.astype(BF16).astype(F32)
    middle = (loss_here - high).astype(BF16).astype(F32)
    low = loss_here - high - middle
    place = lax.broadcasted_iota(jnp.int32, (16, 128), 0)
    pieces = jnp.where(place == 0, high, jnp.where(place == 1, middle, jnp.where(place == 2, low, 0.0)))
    dot_send[0:TILES] = dots[...].astype(BF16)
    dot_send[TILES : TILES + 16] = pieces.astype(BF16)
    dot_recv[grp] = dot_send[...]

    def dot_start(step, carry):
        peer = grp_peer(step)
        remote(dot_send, dot_recv.at[grp], dot_ss.at[step], dot_rs.at[grp], (peer, proto)).start()
        return carry

    lax.fori_loop(1, GRP, dot_start, 0)

    target_unit = unit_finish(1)
    my_rows = own_rows(x_lo * RING + z)
    unit_grad = soft_unit - target_unit * row_wide[my_rows, 0:1]
    wide, scaling = unit_rows(student_in[my_rows, :])
    row_dots = jnp.sum(wide * unit_grad, axis=1, keepdims=True)
    student_out[my_rows, :] = ((unit_grad - wide * row_dots) * scaling).astype(BF16)

    def out_copy(step, owner):
        peer = z_peer(step)
        rows = own_rows(x_lo * RING + owner)
        return remote(
            student_out.at[rows],
            student_out.at[rows],
            outz_ss.at[step],
            outz_rs.at[owner],
            (grp, x_lo * RING + peer),
        )

    def forward(index, owner):
        rows = own_rows(index * RING + owner)
        return remote(student_out.at[rows], student_out.at[rows], outx_ss.at[owner], outx_rs.at[owner], partner_x)

    each_z(lambda step: out_copy(step, z).start())
    forward(x_lo, z).start()

    def dot_wait(step, carry):
        peer = grp_peer(step)
        remote(dot_send, dot_recv.at[peer], dot_ss.at[step], dot_rs.at[peer], (peer, proto)).wait()
        return carry

    lax.fori_loop(1, GRP, dot_wait, 0)
    total = dot_recv[0].astype(F32)
    for peer in range(1, GRP):
        total = total + dot_recv[peer].astype(F32)
    dots[...] = total[0:TILES]
    loss_out[...] = total[TILES : TILES + 1] + total[TILES + 1 : TILES + 2] + total[TILES + 2 : TILES + 3]

    def pass_on(step):
        peer = z_peer(step)
        out_copy(step, peer).wait_recv()
        forward(x_lo, peer).start()

    def pass_pair(step, carry):
        pass_on(step)
        pass_on(RING - step)
        return carry

    lax.fori_loop(1, RING // 2, pass_pair, 0)
    pass_on(RING // 2)

    def term_finish(block, carry):
        cols = columns(block, TERM_BLOCK)

        def wait(step, total):
            peer = chip_peer(step)
            remote(
                term_send.at[block, peer],
                term_recv.at[block, peer],
                term_ss.at[block, step],
                term_rs.at[block, peer],
                (peer * 2 + core, proto),
            ).wait()
            return total + term_recv[block, peer].astype(F32)

        total = lax.fori_loop(1, CHIPS, wait, term_mine[block, chip])
        scaling = proto_scale[:, cols]
        wide = proto_in[pl.ds(pl.multiple_of(grp * SHARE, SHARE), SHARE), cols].astype(F32) * scaling
        dot = jnp.concatenate(
            [dots[pl.ds(block * (TERM_BLOCK // 128) + tile, 1), :] for tile in range(TERM_BLOCK // 128)], axis=1
        )
        proto_out[:, cols] = ((total - wide * dot) * scaling).astype(BF16)
        return carry

    lax.fori_loop(0, TERM_BLOCKS, term_finish, 0)

    def out_wait(step, carry):
        out_copy(step, z).wait_send()
        return carry

    lax.fori_loop(1, RING, out_wait, 0)

    def forward_wait(owner, carry):
        forward(x_lo, owner).wait_send()
        forward(1 - x_lo, owner).wait_recv()
        return carry

    lax.fori_loop(0, RING, forward_wait, 0)


def hand_out(proto_in, student_in, proto_out, student_out, sems):
    copies = [
        pltpu.make_async_copy(proto_in, proto_out, sems.at[0]),
        pltpu.make_async_copy(student_in, student_out, sems.at[1]),
    ]
    for copy in copies:
        copy.start()
    for copy in copies:
        copy.wait()


def per_device(teacher_features, student_features, prototypes):
    vmem = pltpu.VMEM
    dma = pltpu.SemaphoreType.DMA
    proto_grad, student_grad, loss = pl.pallas_call(
        kernel,
        out_shape=(
            jax.ShapeDtypeStruct((SHARE, COLS), BF16),
            jax.ShapeDtypeStruct((ROWS, WIDTH), BF16),
            jax.ShapeDtypeStruct((1, 128), F32),
        ),
        in_specs=[pl.BlockSpec(memory_space=pl.ANY)] * 3,
        out_specs=(pl.BlockSpec(memory_space=vmem),) * 3,
        scratch_shapes=[
            vmem((ROWS, WIDTH), BF16),
            vmem((ROWS, WIDTH), BF16),
            vmem((WIDTH, COLS), BF16),
            vmem((ROWS, WIDTH), BF16),
            vmem((WIDTH, ROWS), BF16),
            vmem((WIDTH, COLS), BF16),
            vmem((COLS, WIDTH), BF16),
            vmem((1, COLS), F32),
            vmem((ROWS, COLS), F32),
            vmem((ROWS, COLS), F32),
            vmem((ROWS, COLS), BF16),
            vmem((ROWS, COLS), BF16),
            vmem((ROWS, 128), F32),
            vmem((TILES, 128), F32),
            vmem((ITERS, TILES, 128), BF16),
            vmem((ITERS, GRP, TILES, 128), BF16),
            vmem((TILES, 128), F32),
            vmem((ITERS, 8, 128), F32),
            vmem((ITERS, 8, 128), F32),
            vmem((ITERS, RING, 8, 128), F32),
            vmem((4, 128), F32),
            vmem((4, 128), F32),
            vmem((RING, 4, 128), F32),
            vmem((ROWS, WIDTH), F32),
            vmem((2, ROWS // 2, WIDTH), BF16),
            vmem((2, ROWS // 2, WIDTH), BF16),
            vmem((2, ROWS // 2, WIDTH), BF16),
            vmem((2, ROWS // 2, WIDTH), F32),
            vmem((2, RING, OWN, WIDTH), BF16),
            vmem((CHIPS, 2, SHARE, TERM_BLOCK), F32),
            vmem((TERM_BLOCKS, CHIPS, SHARE, TERM_BLOCK), BF16),
            vmem((TERM_BLOCKS, CHIPS, SHARE, TERM_BLOCK), BF16),
            vmem((TERM_BLOCKS, CHIPS, SHARE, TERM_BLOCK), F32),
            vmem((TERM_BLOCKS, CHIPS, SHARE, TERM_BLOCK), BF16),
            vmem((TERM_BLOCKS, CHIPS, SHARE, TERM_BLOCK), BF16),
            vmem((TILES, 128), F32),
            vmem((TILES + 16, 128), BF16),
            vmem((GRP, TILES + 16, 128), BF16),
            dma((2 + BLOCKS,)),
            dma((ITERS, GRP)),
            dma((ITERS, GRP)),
            dma((ITERS,)),
            dma((ITERS,)),
            dma((ITERS, RING)),
            dma((ITERS, RING)),
            dma,
            dma,
            dma((RING,)),
            dma((RING,)),
            dma((2,)),
            dma((2,)),
            dma((2, RING)),
            dma((2, RING)),
            dma((RING,)),
            dma((RING,)),
            dma((RING,)),
            dma((RING,)),
            dma((TERM_BLOCKS,)),
            dma((TERM_BLOCKS,)),
            dma((TERM_BLOCKS, CHIPS)),
            dma((TERM_BLOCKS, CHIPS)),
            dma((GRP,)),
            dma((GRP,)),
        ],
        compiler_params=pltpu.CompilerParams(
            collective_id=0, has_side_effects=True, vmem_limit_bytes=56 * 2**20
        ),
        name="sinkhorn_step",
    )(teacher_features, student_features, prototypes)
    proto_grad, student_grad = pl.pallas_call(
        hand_out,
        out_shape=(
            jax.ShapeDtypeStruct((SHARE, COLS), BF16),
            jax.ShapeDtypeStruct((ROWS, WIDTH), BF16),
        ),
        in_specs=[pl.BlockSpec(memory_space=pltpu.HBM)] * 2,
        out_specs=(pl.BlockSpec(memory_space=pltpu.HBM),) * 2,
        scratch_shapes=[dma((2,))],
        name="hand_out",
    )(proto_grad, student_grad)
    return proto_grad, student_grad, loss[0, 0]


def solution(mesh):
    placed = (P("grp", None), P("grp", None), P(None, "proto"))
    return jax.shard_map(
        per_device,
        mesh=mesh,
        in_specs=placed,
        out_specs=(P("grp", "proto"), P("grp", None), P()),
        check_vma=False,
    )
```

```python
import functools
import math

import jax
import jax.numpy as jnp
from jax import lax
from jax.experimental import pallas as pl
from jax.experimental.pallas import tpu as pltpu
from jax.sharding import PartitionSpec as P

MESH = pl.DeviceIdType.MESH
F32 = jnp.float32
BF16 = jnp.bfloat16

ITERS = 3
TEACHER_TEMP = 0.07
STUDENT_TEMP = 0.1
EPSILON = 1e-06
LOG2E = math.log2(math.e)

ROWS = 512
COLS = 4096
WIDTH = 256
GRP = 16
RING = 16
ALL_ROWS = ROWS * GRP
ALL_COLS = COLS * 2 * RING
BLOCK = 512
BLOCKS = COLS // BLOCK
TILES = COLS // 128
TERM_BLOCK = 1024
TERM_BLOCKS = COLS // TERM_BLOCK
HALF_ROWS = ROWS // 2
NEAR = 5
FAR = RING - 1 - 2 * NEAR
SHARE = WIDTH // GRP
CHIPS = 8
OWN = ROWS // (2 * RING)


def lane_broadcast(vector):
    parts = []
    for group in range(4):
        parts.append(jnp.broadcast_to(vector[group : group + 1, :], (128, 128)).T)
    return jnp.concatenate(parts, axis=0)


def fold_lanes(partial):
    parts = []
    for group in range(4):
        block = partial[group * 128 : (group + 1) * 128, :].T
        parts.append(jnp.sum(block, axis=0, keepdims=True))
    return jnp.concatenate(parts, axis=0)


def kernel(
    teacher_hbm,
    student_hbm,
    proto_hbm,
    proto_out,
    student_out,
    loss_out,
    teacher_in,
    student_in,
    proto_in,
    student_unit,
    student_turned,
    proto_unit,
    proto_turned,
    proto_scale,
    exps,
    soft,
    soft_half,
    target_half,
    row_wide,
    col_sums,
    col_send,
    col_recv,
    col_scale,
    row_send,
    row_pair,
    row_recv,
    row_far,
    loss_row,
    loss_pair,
    loss_recv,
    unit_part,
    unit_send,
    unit_pair,
    unit_share,
    unit_recv,
    term,
    core_send,
    core_recv,
    term_mine,
    term_send,
    term_recv,
    dots,
    dot_send,
    dot_recv,
    in_sem,
    col_sem,
    row_x_sem,
    row_near_sem,
    row_far_sem,
    loss_sem,
    unit_x_sem,
    unit_z_sem,
    out_sem,
    core_sem,
    term_sem,
    dot_sem,
):
    grp = lax.axis_index("grp")
    proto = lax.axis_index("proto")
    core = lax.rem(grp, 2)
    chip = lax.div(grp, 2)
    x_lo = lax.div(proto, RING)
    z = lax.rem(proto, RING)
    partner_core = (grp + 1 - 2 * core, proto)
    partner_x = (grp, z + (1 - x_lo) * RING)
    here = x_lo * RING
    across = RING - here

    def grp_peer(step):
        return lax.rem(grp + step, GRP)

    def z_peer(step):
        return lax.rem(z + step, RING)

    def chip_peer(step):
        return lax.rem(chip + step, CHIPS)

    def near_steps(visit):
        def pair(step, carry):
            visit(NEAR + 1 - step)
            visit(RING - NEAR - 1 + step)
            return carry

        lax.fori_loop(1, NEAR + 1, pair, 0)

    def far_steps(visit):
        visit(RING // 2)

        def pair(step, carry):
            visit(RING // 2 - step)
            visit(RING // 2 + step)
            return carry

        lax.fori_loop(1, FAR // 2 + 1, pair, 0)

    def remote(src, dst, sem, device):
        return pltpu.make_async_remote_copy(
            src_ref=src,
            dst_ref=dst,
            send_sem=sem.at[0],
            recv_sem=sem.at[1],
            device_id=device,
            device_id_type=MESH,
        )

    def landed(ref, sem):
        remote(ref, ref, sem, partner_x).wait_recv()

    def left(ref, sem):
        remote(ref, ref, sem, partner_x).wait_send()

    barrier = pltpu.get_barrier_semaphore()

    def greet_grp(step, carry):
        pl.semaphore_signal(barrier, inc=1, device_id=(grp_peer(step), proto), device_id_type=MESH)
        return carry

    def greet_z(step, carry):
        pl.semaphore_signal(barrier, inc=1, device_id=(grp, here + z_peer(step)), device_id_type=MESH)
        return carry

    lax.fori_loop(1, RING, greet_z, 0)
    lax.fori_loop(1, GRP, greet_grp, 0)
    pl.semaphore_signal(barrier, inc=1, device_id=partner_x, device_id_type=MESH)
    far_steps(
        lambda step: pl.semaphore_signal(
            barrier, inc=1, device_id=(grp, across + z_peer(step)), device_id_type=MESH
        )
    )

    loads = [
        pltpu.make_async_copy(teacher_hbm, teacher_in, in_sem.at[0]),
        pltpu.make_async_copy(student_hbm, student_in, in_sem.at[1]),
    ]

    def columns(block, size=BLOCK):
        return pl.ds(pl.multiple_of(block * size, size), size)

    def proto_load(block):
        cols = columns(block)
        return pltpu.make_async_copy(proto_hbm.at[:, cols], proto_in.at[:, cols], in_sem.at[2 + block])

    loads[0].start()
    lax.fori_loop(0, BLOCKS, lambda block, carry: (proto_load(block).start(), carry)[1], 0)
    loads[1].start()

    def unit_rows(features):
        wide = features.astype(F32)
        scaling = lax.rsqrt(jnp.sum(wide * wide, axis=1, keepdims=True) + EPSILON)
        return wide * scaling, scaling

    loads[0].wait()
    teacher_in[...] = unit_rows(teacher_in[...])[0].astype(BF16)

    def teacher_block(block, carry):
        proto_load(block).wait()
        cols = columns(block)
        wide = proto_in[:, cols].astype(F32)
        scaling = lax.rsqrt(jnp.sum(wide * wide, axis=0, keepdims=True) + EPSILON)
        proto_scale[:, cols] = scaling
        unit = (wide * scaling).astype(BF16)
        proto_unit[:, cols] = unit
        product = jnp.dot(teacher_in[...], unit, preferred_element_type=F32)
        values = jnp.exp2(product * (LOG2E / TEACHER_TEMP))
        exps[:, cols] = values
        total = jnp.sum(values, axis=0, keepdims=True)
        for tile in range(BLOCK // 128):
            col_sums[pl.ds(block * (BLOCK // 128) + tile, 1), :] = total[:, tile * 128 : (tile + 1) * 128]
        return carry

    lax.fori_loop(0, BLOCKS, teacher_block, 0)

    pl.semaphore_wait(barrier, GRP - 1 + RING - 1 + 1 + FAR)

    def col_start(turn):
        message = col_sums[...].astype(BF16)
        col_send[turn] = message
        col_recv[turn, GRP - 1] = message

        def send(step, carry):
            remote(
                col_send.at[turn], col_recv.at[turn, GRP - 1 - step], col_sem.at[turn], (grp_peer(step), proto)
            ).start()
            return carry

        lax.fori_loop(1, GRP, send, 0)

    def col_finish(turn):
        arrivals = col_recv.at[turn, pl.ds(0, GRP - 1)]
        landed(arrivals, col_sem.at[turn])
        total = col_recv[turn, 0].astype(F32)
        for slot in range(1, GRP):
            total = total + col_recv[turn, slot].astype(F32)
        col_scale[...] = 1.0 / (ALL_COLS * total)
        left(arrivals, col_sem.at[turn])

    def ring_order(slots):
        total = slots[lax.rem(RING - 1 - z + RING, RING)]
        for index in range(1, RING):
            total = total + slots[lax.rem(index + RING - 1 - z + RING, RING)]
        return total

    def row_refs(turn):
        rows = pl.ds(0, 8 if turn == 0 else 4)
        return (
            row_send.at[turn, rows],
            row_pair.at[turn, 0, rows],
            row_pair.at[turn, 1, rows],
            row_recv.at[turn, :, rows],
            row_far.at[turn, :, rows],
        )

    def row_start(turn):
        send, pair, both, slots, far = row_refs(turn)

        def to_far(step):
            slot = RING // 2 + FAR // 2 - step
            remote(send, far.at[slot], row_far_sem.at[turn], (grp, here + z_peer(step))).start()
            remote(send, far.at[FAR + slot], row_far_sem.at[turn], (grp, across + z_peer(step))).start()

        remote(send, pair, row_x_sem.at[turn], partner_x).start()
        far_steps(to_far)

    def row_ring(turn):
        send, pair, both, slots, far = row_refs(turn)
        landed(pair, row_x_sem.at[turn])
        total = send[...] + pair[...]
        both[...] = total
        slots[RING - 1] = total
        near_steps(
            lambda step: remote(
                both, slots.at[RING - 1 - step], row_near_sem.at[turn], (grp, here + z_peer(step))
            ).start()
        )

    def row_finish(turn):
        send, pair, both, slots, far = row_refs(turn)
        landed(slots.at[pl.ds(0, 2 * NEAR)], row_near_sem.at[turn])
        landed(far, row_far_sem.at[turn])
        for index in range(FAR):
            slots[NEAR + index] = far[index] + far[FAR + index]
        left(pair, row_x_sem.at[turn])
        left(slots.at[pl.ds(0, 2 * NEAR)], row_near_sem.at[turn])
        left(far, row_far_sem.at[turn])
        return ring_order(slots)

    def row_pass():
        def rows_of(block, carry):
            rows = pl.ds(pl.multiple_of(block * 64, 64), 64)
            partial = jnp.zeros((64, 128), F32)
            for tile in range(TILES):
                partial = partial + exps[rows, pl.ds(tile * 128, 128)] * col_scale[pl.ds(tile, 1), :]
            row_wide[rows, :] = partial
            return carry

        lax.fori_loop(0, ROWS // 64, rows_of, 0)
        return fold_lanes(row_wide[...])

    def target_pass():
        def rows_of(block, carry):
            rows = pl.ds(pl.multiple_of(block * 64, 64), 64)
            partial = jnp.zeros((64, 128), F32)
            for tile in range(TILES):
                cols = pl.ds(tile * 128, 128)
                scaled = exps[rows, cols] * col_scale[pl.ds(tile, 1), :]
                target_half[rows, cols] = scaled.astype(BF16)
                partial = partial + scaled
            row_wide[rows, :] = partial
            return carry

        lax.fori_loop(0, ROWS // 64, rows_of, 0)
        return fold_lanes(row_wide[...])

    def col_pass():
        def block_of(block, carry):
            cols = columns(block)
            partial = jnp.zeros((8, BLOCK), F32)
            for group in range(ROWS // 8):
                rows = pl.ds(group * 8, 8)
                scale = row_wide[rows, :]
                partial = partial + exps[rows, cols] * jnp.concatenate([scale] * (BLOCK // 128), axis=1)
            total = jnp.sum(partial, axis=0, keepdims=True)
            for tile in range(BLOCK // 128):
                col_sums[pl.ds(block * (BLOCK // 128) + tile, 1), :] = total[:, tile * 128 : (tile + 1) * 128]
            return carry

        lax.fori_loop(0, BLOCKS, block_of, 0)

    mine = pl.ds(pl.multiple_of(x_lo * HALF_ROWS, HALF_ROWS), HALF_ROWS)
    other = pl.ds(pl.multiple_of((1 - x_lo) * HALF_ROWS, HALF_ROWS), HALF_ROWS)

    def unit_matmul(source, rows):
        unit_part[rows, :] = jnp.dot(source[rows, :], proto_turned[...], preferred_element_type=F32)

    def own_rows(index):
        return pl.ds(pl.multiple_of(index * OWN, OWN), OWN)

    near_rows = pl.ds(0, (2 * NEAR + 1) * OWN)

    def unit_x(part):
        unit_send[part] = unit_part[...].astype(BF16)

        def send(step, carry):
            rows = own_rows(lax.rem(z + step + RING - NEAR, RING))
            theirs = own_rows(across + lax.rem(z + step + RING - NEAR, RING))
            remote(unit_send.at[part, theirs], unit_pair.at[part, rows], unit_x_sem.at[part], partner_x).start()
            return carry

        lax.fori_loop(0, 2 * NEAR + 1, send, 0)

    def unit_far(part):
        def to_far(step):
            peer = z_peer(step)
            slot = 2 * NEAR + RING // 2 + FAR // 2 - step
            remote(
                unit_send.at[part, own_rows(across + peer)],
                unit_recv.at[part, FAR + slot],
                unit_z_sem.at[part],
                (grp, across + peer),
            ).start()
            remote(
                unit_send.at[part, own_rows(here + peer)],
                unit_recv.at[part, slot],
                unit_z_sem.at[part],
                (grp, here + peer),
            ).start()

        far_steps(to_far)

    def unit_near(part):
        landed(unit_pair.at[part, near_rows], unit_x_sem.at[part])

        def to_near(step):
            peer = z_peer(step)
            rows = own_rows(peer)
            total = unit_part[own_rows(here + peer), :] + unit_pair[part, rows, :].astype(F32)
            unit_share[part, rows, :] = total.astype(BF16)
            slot = step - 1 - NEAR * lax.div(step, RING // 2)
            remote(
                unit_share.at[part, rows], unit_recv.at[part, slot], unit_z_sem.at[part], (grp, here + peer)
            ).start()

        near_steps(to_near)

    def unit_own(part):
        return unit_part[own_rows(here + z), :] + unit_pair[part, own_rows(z), :].astype(F32)

    def unit_finish(part, total):
        landed(unit_recv.at[part], unit_z_sem.at[part])
        for slot in range(2 * NEAR + 2 * FAR):
            total = total + unit_recv[part, slot].astype(F32)
        left(unit_pair.at[part, near_rows], unit_x_sem.at[part])
        left(unit_recv.at[part], unit_z_sem.at[part])
        return total

    col_start(0)
    loads[1].wait()
    student_unit[...] = unit_rows(student_in[...])[0].astype(BF16)

    def student_block(block, carry):
        cols = columns(block)
        product = jnp.dot(student_unit[...], proto_unit[:, cols], preferred_element_type=F32)
        values = jnp.exp2(product * (LOG2E / STUDENT_TEMP))
        soft[:, cols] = values
        partial = values[:, :128]
        for tile in range(1, BLOCK // 128):
            partial = partial + values[:, tile * 128 : (tile + 1) * 128]
        row_wide[...] = row_wide[...] + partial
        return carry

    row_wide[...] = jnp.zeros((ROWS, 128), F32)
    lax.fori_loop(0, BLOCKS, student_block, 0)
    row_send[0, 4:8] = fold_lanes(row_wide[...])
    col_finish(0)
    row_send[0, 0:4] = row_pass()
    row_start(0)
    student_turned[...] = student_unit[...].astype(F32).T.astype(BF16)
    row_ring(0)

    def turn_block(block, carry):
        cols = columns(block)
        proto_turned[cols, :] = proto_unit[:, cols].T
        return carry

    lax.fori_loop(0, BLOCKS, turn_block, 0)
    sums = row_finish(0)
    row_scale = 1.0 / (ALL_ROWS * sums[0:4])
    student_total = sums[4:8]

    row_wide[...] = lane_broadcast(row_scale)
    col_pass()
    col_start(1)
    row_wide[...] = lane_broadcast((1.0 / STUDENT_TEMP) / student_total)

    def soft_rows(block, carry):
        rows = pl.ds(pl.multiple_of(block * 64, 64), 64)
        scale = row_wide[rows, :]
        for tile in range(TILES):
            cols = pl.ds(tile * 128, 128)
            soft_half[rows, cols] = (soft[rows, cols] * scale).astype(BF16)
        return carry

    lax.fori_loop(0, ROWS // 64, soft_rows, 0)
    unit_matmul(soft_half, pl.ds(0, ROWS))
    col_finish(1)
    row_send[1, 0:4] = row_pass()
    row_start(1)
    row_ring(1)
    unit_x(0)
    row_scale = 1.0 / (ALL_ROWS * row_finish(1))

    row_wide[...] = lane_broadcast(row_scale)
    col_pass()
    col_start(2)
    unit_far(0)
    unit_near(0)
    soft_own = unit_own(0)
    col_finish(2)
    row_send[2, 0:4] = target_pass()
    row_start(2)
    unit_matmul(target_half, pl.ds(0, ROWS))
    unit_x(1)
    unit_far(1)
    row_ring(2)
    row_wide[...] = unit_part[:, :128] * student_unit[:, :128].astype(F32) + unit_part[:, 128:] * student_unit[
        :, 128:
    ].astype(F32)
    loss_row[0] = fold_lanes(row_wide[...])
    remote(loss_row.at[0], loss_pair, loss_sem.at[0], partner_x).start()
    unit_near(1)
    target_own = unit_own(1)
    landed(loss_pair, loss_sem.at[0])
    loss_row[1] = loss_row[0] + loss_pair[...]
    loss_recv[RING - 1] = loss_row[1]

    def loss_send(step, carry):
        remote(
            loss_row.at[1], loss_recv.at[RING - 1 - step], loss_sem.at[1], (grp, here + z_peer(step))
        ).start()
        return carry

    lax.fori_loop(1, RING, loss_send, 0)
    soft_unit = unit_finish(0, soft_own)
    row_scale = 1.0 / (ALL_ROWS * row_finish(2))
    row_wide[...] = lane_broadcast((ALL_ROWS / STUDENT_TEMP) * row_scale)

    def core_copy(block):
        return remote(core_send.at[block], core_recv.at[block], core_sem.at[block], partner_core)

    def term_ring(block):
        core_copy(block).wait()
        total = term_mine[block] + core_recv[block].astype(F32)
        term_mine[block] = total
        term_send[block] = total.astype(BF16)

        def send(step, carry):
            peer = chip_peer(step)
            remote(
                term_send.at[block, peer],
                term_recv.at[block, CHIPS - 1 - step],
                term_sem.at[block],
                (peer * 2 + core, proto),
            ).start()
            return carry

        lax.fori_loop(1, CHIPS, send, 0)

    def term_block(block, carry):
        cols = columns(block, TERM_BLOCK)
        scale = jnp.concatenate([row_wide[...]] * (TERM_BLOCK // 128), axis=1)
        dlogits = (soft_half[:, cols].astype(F32) - target_half[:, cols].astype(F32) * scale).astype(BF16)
        product = jnp.dot(student_turned[...], dlogits, preferred_element_type=F32)
        term[...] = product.reshape(CHIPS, 2, SHARE, TERM_BLOCK)
        core_send[block] = term[:, 1 - core].astype(BF16)
        core_copy(block).start()
        term_mine[block] = term[:, core]
        total = jnp.sum(product * proto_in[:, cols].astype(F32), axis=0, keepdims=True) * proto_scale[:, cols]
        for tile in range(TERM_BLOCK // 128):
            dots[pl.ds(block * (TERM_BLOCK // 128) + tile, 1), :] = total[:, tile * 128 : (tile + 1) * 128]

        @pl.when(block > 0)
        def _():
            term_ring(block - 1)

        return carry

    lax.fori_loop(0, TERM_BLOCKS, term_block, 0)
    term_ring(TERM_BLOCKS - 1)
    landed(loss_recv.at[pl.ds(0, RING - 1)], loss_sem.at[1])
    agreement = (ALL_ROWS / STUDENT_TEMP) * row_scale * ring_order(loss_recv)
    left(loss_pair, loss_sem.at[0])
    left(loss_recv.at[pl.ds(0, RING - 1)], loss_sem.at[1])
    loss_here = jnp.sum(jnp.log(student_total) - agreement) * (1.0 / ALL_ROWS)

    high = loss_here.astype(BF16).astype(F32)
    middle = (loss_here - high).astype(BF16).astype(F32)
    low = loss_here - high - middle
    place = lax.broadcasted_iota(jnp.int32, (16, 128), 0)
    pieces = jnp.where(place == 0, high, jnp.where(place == 1, middle, jnp.where(place == 2, low, 0.0)))
    dot_send[0:TILES] = dots[...].astype(BF16)
    dot_send[TILES : TILES + 16] = pieces.astype(BF16)
    dot_recv[GRP - 1] = dot_send[...]

    def dot_start(step, carry):
        remote(dot_send, dot_recv.at[GRP - 1 - step], dot_sem, (grp_peer(step), proto)).start()
        return carry

    lax.fori_loop(1, GRP, dot_start, 0)

    target_unit = unit_finish(1, target_own)
    my_rows = own_rows(here + z)
    unit_grad = soft_unit - target_unit * row_wide[my_rows, 0:1]
    wide, scaling = unit_rows(student_in[my_rows, :])
    row_dots = jnp.sum(wide * unit_grad, axis=1, keepdims=True)
    student_out[my_rows, :] = ((unit_grad - wide * row_dots) * scaling).astype(BF16)

    def out_send(step, base, sem):
        rows = student_out.at[my_rows]
        remote(rows, rows, sem, (grp, base + z_peer(step))).start()

    def out_far(step):
        out_send(step, across, out_sem.at[1])
        out_send(step, here, out_sem.at[1])

    def forward(owner):
        rows = student_out.at[own_rows(here + owner)]
        remote(rows, rows, out_sem.at[2], partner_x).start()

    far_steps(out_far)
    near_steps(lambda step: out_send(step, here, out_sem.at[0]))
    forward(z)

    dot_arrivals = dot_recv.at[pl.ds(0, GRP - 1)]
    landed(dot_arrivals, dot_sem)
    total = jnp.zeros((TILES + 16, 128), F32)
    for index in range(GRP):
        total = total + dot_recv[lax.rem(index + GRP - 1 - grp + GRP, GRP)].astype(F32)
    dots[...] = total[0:TILES]
    loss_out[...] = total[TILES : TILES + 1] + total[TILES + 1 : TILES + 2] + total[TILES + 2 : TILES + 3]
    left(dot_arrivals, dot_sem)

    near_out = student_out.at[pl.ds(0, 2 * NEAR * OWN)]
    landed(near_out, out_sem.at[0])
    near_steps(lambda step: forward(z_peer(step)))

    def term_finish(block, carry):
        cols = columns(block, TERM_BLOCK)

        arrivals = term_recv.at[block]
        landed(arrivals, term_sem.at[block])
        total = term_mine[block, chip]
        for slot in range(CHIPS - 1):
            total = total + term_recv[block, slot].astype(F32)
        left(arrivals, term_sem.at[block])
        scaling = proto_scale[:, cols]
        wide = proto_in[pl.ds(pl.multiple_of(grp * SHARE, SHARE), SHARE), cols].astype(F32) * scaling
        dot = jnp.concatenate(
            [dots[pl.ds(block * (TERM_BLOCK // 128) + tile, 1), :] for tile in range(TERM_BLOCK // 128)], axis=1
        )
        proto_out[:, cols] = ((total - wide * dot) * scaling).astype(BF16)
        return carry

    lax.fori_loop(0, TERM_BLOCKS, term_finish, 0)

    far_out = student_out.at[pl.ds(0, 2 * FAR * OWN)]
    passed_out = student_out.at[pl.ds(0, (2 * NEAR + 1) * OWN)]
    landed(far_out, out_sem.at[1])
    landed(passed_out, out_sem.at[2])
    left(near_out, out_sem.at[0])
    left(far_out, out_sem.at[1])
    left(passed_out, out_sem.at[2])


def per_device(teacher_features, student_features, prototypes):
    vmem = pltpu.VMEM
    dma = pltpu.SemaphoreType.DMA
    proto_grad, student_grad, loss = pl.pallas_call(
        kernel,
        out_shape=(
            vmem((SHARE, COLS), BF16),
            vmem((ROWS, WIDTH), BF16),
            jax.ShapeDtypeStruct((1, 128), F32),
        ),
        in_specs=[pl.BlockSpec(memory_space=pl.ANY)] * 3,
        out_specs=(pl.BlockSpec(memory_space=vmem),) * 3,
        scratch_shapes=[
            vmem((ROWS, WIDTH), BF16),
            vmem((ROWS, WIDTH), BF16),
            vmem((WIDTH, COLS), BF16),
            vmem((ROWS, WIDTH), BF16),
            vmem((WIDTH, ROWS), BF16),
            vmem((WIDTH, COLS), BF16),
            vmem((COLS, WIDTH), BF16),
            vmem((1, COLS), F32),
            vmem((ROWS, COLS), F32),
            vmem((ROWS, COLS), F32),
            vmem((ROWS, COLS), BF16),
            vmem((ROWS, COLS), BF16),
            vmem((ROWS, 128), F32),
            vmem((TILES, 128), F32),
            vmem((ITERS, TILES, 128), BF16),
            vmem((ITERS, GRP, TILES, 128), BF16),
            vmem((TILES, 128), F32),
            vmem((ITERS, 8, 128), F32),
            vmem((ITERS, 2, 8, 128), F32),
            vmem((ITERS, RING, 8, 128), F32),
            vmem((ITERS, 2 * FAR, 8, 128), F32),
            vmem((2, 4, 128), F32),
            vmem((4, 128), F32),
            vmem((RING, 4, 128), F32),
            vmem((ROWS, WIDTH), F32),
            vmem((2, ROWS, WIDTH), BF16),
            vmem((2, HALF_ROWS, WIDTH), BF16),
            vmem((2, HALF_ROWS, WIDTH), BF16),
            vmem((2, 2 * NEAR + 2 * FAR, OWN, WIDTH), BF16),
            vmem((CHIPS, 2, SHARE, TERM_BLOCK), F32),
            vmem((TERM_BLOCKS, CHIPS, SHARE, TERM_BLOCK), BF16),
            vmem((TERM_BLOCKS, CHIPS, SHARE, TERM_BLOCK), BF16),
            vmem((TERM_BLOCKS, CHIPS, SHARE, TERM_BLOCK), F32),
            vmem((TERM_BLOCKS, CHIPS, SHARE, TERM_BLOCK), BF16),
            vmem((TERM_BLOCKS, CHIPS - 1, SHARE, TERM_BLOCK), BF16),
            vmem((TILES, 128), F32),
            vmem((TILES + 16, 128), BF16),
            vmem((GRP, TILES + 16, 128), BF16),
            dma((2 + BLOCKS,)),
            dma((ITERS, 2)),
            dma((ITERS, 2)),
            dma((ITERS, 2)),
            dma((ITERS, 2)),
            dma((2, 2)),
            dma((2, 2)),
            dma((2, 2)),
            dma((3, 2)),
            dma((TERM_BLOCKS, 2)),
            dma((TERM_BLOCKS, 2)),
            dma((2,)),
        ],
        compiler_params=pltpu.CompilerParams(
            collective_id=0, has_side_effects=True, vmem_limit_bytes=56 * 2**20
        ),
        name="sinkhorn_step",
    )(teacher_features, student_features, prototypes)
    return proto_grad, student_grad, loss[0, 0]


def solution(mesh):
    placed = (P("grp", None), P("grp", None), P(None, "proto"))
    return jax.shard_map(
        per_device,
        mesh=mesh,
        in_specs=placed,
        out_specs=(P("grp", "proto"), P("grp", None), P()),
        check_vma=False,
    )
```

```python
import functools
import math

import jax
import jax.numpy as jnp
from jax import lax
from jax.experimental import pallas as pl
from jax.experimental.pallas import tpu as pltpu
from jax.sharding import PartitionSpec as P

MESH = pl.DeviceIdType.MESH
F32 = jnp.float32
BF16 = jnp.bfloat16

ITERS = 3
TEACHER_TEMP = 0.07
STUDENT_TEMP = 0.1
EPSILON = 1e-06
LOG2E = math.log2(math.e)

ROWS = 512
COLS = 4096
WIDTH = 256
GRP = 16
RING = 16
ALL_ROWS = ROWS * GRP
ALL_COLS = COLS * 2 * RING
BLOCK = 512
BLOCKS = COLS // BLOCK
TILES = COLS // 128
TERM_BLOCK = 512
TERM_BLOCKS = COLS // TERM_BLOCK
HALF_ROWS = ROWS // 2
NEAR = 5
FAR = RING - 1 - 2 * NEAR
SHARE = WIDTH // GRP
CHIPS = 8
OWN = ROWS // (2 * RING)


def lane_broadcast(vector):
    parts = []
    for group in range(4):
        parts.append(jnp.broadcast_to(vector[group : group + 1, :], (128, 128)).T)
    return jnp.concatenate(parts, axis=0)


def fold_lanes(partial):
    parts = []
    for group in range(4):
        block = partial[group * 128 : (group + 1) * 128, :].T
        parts.append(jnp.sum(block, axis=0, keepdims=True))
    return jnp.concatenate(parts, axis=0)


def kernel(
    teacher_hbm,
    student_hbm,
    proto_hbm,
    proto_out,
    student_out,
    loss_out,
    teacher_in,
    student_in,
    proto_in,
    student_unit,
    student_turned,
    proto_unit,
    proto_turned,
    proto_scale,
    exps,
    soft,
    soft_half,
    target_half,
    row_wide,
    col_sums,
    col_send,
    col_recv,
    col_scale,
    row_send,
    row_recv,
    loss_row,
    loss_pair,
    loss_recv,
    loss_send,
    loss_all,
    unit_part,
    unit_send,
    unit_pair,
    unit_share,
    unit_recv,
    term,
    core_send,
    core_recv,
    term_mine,
    term_send,
    term_recv,
    dots,
    dot_send,
    dot_recv,
    in_sem,
    col_sem,
    row_sem,
    loss_sem,
    unit_x_sem,
    unit_z_sem,
    out_sem,
    core_sem,
    term_sem,
    dot_sem,
):
    grp = lax.axis_index("grp")
    proto = lax.axis_index("proto")
    core = lax.rem(grp, 2)
    chip = lax.div(grp, 2)
    x_lo = lax.div(proto, RING)
    z = lax.rem(proto, RING)
    partner_core = (grp + 1 - 2 * core, proto)
    partner_x = (grp, z + (1 - x_lo) * RING)
    here = x_lo * RING
    across = RING - here

    def grp_peer(step):
        return lax.rem(grp + step, GRP)

    def z_peer(step):
        return lax.rem(z + step, RING)

    def chip_peer(step):
        return lax.rem(chip + step, CHIPS)

    def near_steps(visit):
        def pair(step, carry):
            visit(NEAR + 1 - step)
            visit(RING - NEAR - 1 + step)
            return carry

        lax.fori_loop(1, NEAR + 1, pair, 0)

    def far_steps(visit):
        visit(RING // 2)

        def pair(step, carry):
            visit(RING // 2 - step)
            visit(RING // 2 + step)
            return carry

        lax.fori_loop(1, FAR // 2 + 1, pair, 0)

    def remote(src, dst, sem, device):
        return pltpu.make_async_remote_copy(
            src_ref=src,
            dst_ref=dst,
            send_sem=sem.at[0],
            recv_sem=sem.at[1],
            device_id=device,
            device_id_type=MESH,
        )

    def landed(ref, sem):
        remote(ref, ref, sem, partner_x).wait_recv()

    def left(ref, sem):
        remote(ref, ref, sem, partner_x).wait_send()

    loads = [
        pltpu.make_async_copy(teacher_hbm, teacher_in, in_sem.at[0]),
        pltpu.make_async_copy(student_hbm, student_in, in_sem.at[1]),
    ]

    def columns(block, size=BLOCK):
        return pl.ds(pl.multiple_of(block * size, size), size)

    def proto_load(block):
        cols = columns(block)
        return pltpu.make_async_copy(proto_hbm.at[:, cols], proto_in.at[:, cols], in_sem.at[2 + block])

    loads[0].start()
    lax.fori_loop(0, BLOCKS, lambda block, carry: (proto_load(block).start(), carry)[1], 0)
    loads[1].start()

    barrier = pltpu.get_barrier_semaphore()

    def greet_grp(step, carry):
        pl.semaphore_signal(barrier, inc=1, device_id=(grp_peer(step), proto), device_id_type=MESH)
        return carry

    def greet_proto(step, carry):
        pl.semaphore_signal(barrier, inc=1, device_id=(grp, lax.rem(proto + step, 2 * RING)), device_id_type=MESH)
        return carry

    lax.fori_loop(1, 2 * RING, greet_proto, 0)
    lax.fori_loop(1, GRP, greet_grp, 0)

    def unit_rows(features):
        wide = features.astype(F32)
        scaling = lax.rsqrt(jnp.sum(wide * wide, axis=1, keepdims=True) + EPSILON)
        return wide * scaling, scaling

    loads[0].wait()
    teacher_in[...] = unit_rows(teacher_in[...])[0].astype(BF16)

    def teacher_block(block, carry):
        proto_load(block).wait()
        cols = columns(block)
        wide = proto_in[:, cols].astype(F32)
        scaling = lax.rsqrt(jnp.sum(wide * wide, axis=0, keepdims=True) + EPSILON)
        proto_scale[:, cols] = scaling
        unit = (wide * scaling).astype(BF16)
        proto_unit[:, cols] = unit
        product = jnp.dot(teacher_in[...], unit, preferred_element_type=F32)
        values = jnp.exp2(product * (LOG2E / TEACHER_TEMP))
        exps[:, cols] = values
        total = jnp.sum(values, axis=0, keepdims=True)
        for tile in range(BLOCK // 128):
            col_sums[pl.ds(block * (BLOCK // 128) + tile, 1), :] = total[:, tile * 128 : (tile + 1) * 128]
        return carry

    lax.fori_loop(0, BLOCKS, teacher_block, 0)

    pl.semaphore_wait(barrier, GRP - 1 + 2 * RING - 1)

    def col_start(turn):
        message = col_sums[...].astype(BF16)
        col_send[turn] = message
        col_recv[turn, GRP - 1] = message

        def send(step, carry):
            remote(
                col_send.at[turn], col_recv.at[turn, GRP - 1 - step], col_sem.at[turn], (grp_peer(step), proto)
            ).start()
            return carry

        lax.fori_loop(1, GRP, send, 0)

    def col_finish(turn):
        arrivals = col_recv.at[turn, pl.ds(0, GRP - 1)]
        landed(arrivals, col_sem.at[turn])
        total = col_recv[turn, 0].astype(F32)
        for slot in range(1, GRP):
            total = total + col_recv[turn, slot].astype(F32)
        col_scale[...] = 1.0 / (ALL_COLS * total)
        left(arrivals, col_sem.at[turn])

    PEERS = 2 * RING - 1

    def ring_order(slots):
        total = slots[lax.rem(RING - 1 - z + RING, RING)]
        for index in range(1, RING):
            total = total + slots[lax.rem(index + RING - 1 - z + RING, RING)]
        return total

    def row_start(turn, sums):
        row_send[turn] = sums
        row_recv[turn, PEERS] = sums

        def send(step, base, offset):
            remote(
                row_send.at[turn],
                row_recv.at[turn, PEERS - offset - step],
                row_sem.at[turn],
                (grp, base + z_peer(step)),
            ).start()

        def four(step, carry):
            for base, offset in ((here, 0), (across, RING)):
                send(RING // 2 - step, base, offset)
                send(RING // 2 + step, base, offset)
            return carry

        send(RING // 2, across, RING)
        send(RING // 2, here, 0)
        lax.fori_loop(1, RING // 2, four, 0)
        send(0, across, RING)

    def row_finish(turn):
        arrivals = row_recv.at[turn, pl.ds(0, PEERS)]
        landed(arrivals, row_sem.at[turn])
        total = None
        for index in range(RING):
            slot = lax.rem(index + RING - 1 - z + RING, RING)
            own = row_recv[turn, RING + slot]
            other = row_recv[turn, slot]
            total = own + other if total is None else total + (own + other)
        left(arrivals, row_sem.at[turn])
        return total

    def row_pass():
        def rows_of(block, carry):
            rows = pl.ds(pl.multiple_of(block * 64, 64), 64)
            partial = jnp.zeros((64, 128), F32)
            for tile in range(TILES):
                partial = partial + exps[rows, pl.ds(tile * 128, 128)] * col_scale[pl.ds(tile, 1), :]
            row_wide[rows, :] = partial
            return carry

        lax.fori_loop(0, ROWS // 64, rows_of, 0)
        return fold_lanes(row_wide[...])

    def target_pass():
        def rows_of(block, carry):
            rows = pl.ds(pl.multiple_of(block * 64, 64), 64)
            partial = jnp.zeros((64, 128), F32)
            for tile in range(TILES):
                cols = pl.ds(tile * 128, 128)
                scaled = exps[rows, cols] * col_scale[pl.ds(tile, 1), :]
                target_half[rows, cols] = scaled.astype(BF16)
                partial = partial + scaled
            row_wide[rows, :] = partial
            return carry

        lax.fori_loop(0, ROWS // 64, rows_of, 0)
        return fold_lanes(row_wide[...])

    def col_pass():
        def block_of(block, carry):
            cols = columns(block)
            partial = jnp.zeros((8, BLOCK), F32)
            for group in range(ROWS // 8):
                rows = pl.ds(group * 8, 8)
                scale = row_wide[rows, :]
                partial = partial + exps[rows, cols] * jnp.concatenate([scale] * (BLOCK // 128), axis=1)
            total = jnp.sum(partial, axis=0, keepdims=True)
            for tile in range(BLOCK // 128):
                col_sums[pl.ds(block * (BLOCK // 128) + tile, 1), :] = total[:, tile * 128 : (tile + 1) * 128]
            return carry

        lax.fori_loop(0, BLOCKS, block_of, 0)

    mine = pl.ds(pl.multiple_of(x_lo * HALF_ROWS, HALF_ROWS), HALF_ROWS)
    other = pl.ds(pl.multiple_of((1 - x_lo) * HALF_ROWS, HALF_ROWS), HALF_ROWS)

    def unit_matmul(source, rows):
        unit_part[rows, :] = jnp.dot(source[rows, :], proto_turned[...], preferred_element_type=F32)

    def own_rows(index):
        return pl.ds(pl.multiple_of(index * OWN, OWN), OWN)

    ring_rows = pl.ds(0, (RING - 1) * OWN)
    near_rows = pl.ds(0, (2 * NEAR + 1) * OWN)

    def soft_x():
        unit_send[0, other, :] = unit_part[other, :].astype(BF16)
        remote(unit_send.at[0, other], unit_pair.at[0], unit_x_sem.at[0], partner_x).start()

    def soft_ring():
        landed(unit_pair.at[0], unit_x_sem.at[0])
        total = unit_part[mine, :] + unit_pair[0].astype(F32)
        unit_share[0] = total.astype(BF16)

        def send(step, carry):
            peer = z_peer(step)
            remote(
                unit_share.at[0, own_rows(peer)], unit_recv.at[0, step - 1], unit_z_sem.at[0], (grp, here + peer)
            ).start()
            return carry

        lax.fori_loop(1, RING, send, 0)

    def soft_finish(total):
        landed(unit_recv.at[0, pl.ds(0, RING - 1)], unit_z_sem.at[0])
        for slot in range(RING - 1):
            total = total + unit_recv[0, slot].astype(F32)
        left(unit_pair.at[0], unit_x_sem.at[0])
        left(unit_share.at[0, ring_rows], unit_z_sem.at[0])
        return total

    def unit_x():
        unit_send[1, other, :] = unit_part[other, :].astype(BF16)

        def send(step, carry):
            owner = lax.rem(z + step + RING - NEAR, RING)
            remote(
                unit_send.at[1, own_rows(across + owner)],
                unit_pair.at[1, own_rows(owner)],
                unit_x_sem.at[1],
                partner_x,
            ).start()
            return carry

        lax.fori_loop(0, 2 * NEAR + 1, send, 0)

    def unit_far(base, offset):
        def to_far(step):
            peer = z_peer(step)
            slot = offset + 2 * NEAR + RING // 2 + FAR // 2 - step
            remote(
                unit_send.at[1, own_rows(base + peer)], unit_recv.at[1, slot], unit_z_sem.at[1], (grp, base + peer)
            ).start()

        far_steps(to_far)

    def unit_near():
        landed(unit_pair.at[1, near_rows], unit_x_sem.at[1])

        def to_near(step):
            peer = z_peer(step)
            rows = own_rows(peer)
            total = unit_part[own_rows(here + peer), :] + unit_pair[1, rows, :].astype(F32)
            unit_share[1, rows, :] = total.astype(BF16)
            slot = step - 1 - NEAR * lax.div(step, RING // 2)
            remote(unit_share.at[1, rows], unit_recv.at[1, slot], unit_z_sem.at[1], (grp, here + peer)).start()

        near_steps(to_near)

    def unit_own(part):
        return unit_part[own_rows(here + z), :] + unit_pair[part, own_rows(z), :].astype(F32)

    def unit_finish(total):
        landed(unit_recv.at[1], unit_z_sem.at[1])
        for slot in range(2 * NEAR + 2 * FAR):
            total = total + unit_recv[1, slot].astype(F32)
        left(unit_pair.at[1, near_rows], unit_x_sem.at[1])
        left(unit_recv.at[1], unit_z_sem.at[1])
        return total

    col_start(0)
    loads[1].wait()
    student_unit[...] = unit_rows(student_in[...])[0].astype(BF16)

    def student_block(block, carry):
        cols = columns(block)
        product = jnp.dot(student_unit[...], proto_unit[:, cols], preferred_element_type=F32)
        values = jnp.exp2(product * (LOG2E / STUDENT_TEMP))
        soft[:, cols] = values
        partial = values[:, :128]
        for tile in range(1, BLOCK // 128):
            partial = partial + values[:, tile * 128 : (tile + 1) * 128]
        row_wide[...] = row_wide[...] + partial
        return carry

    row_wide[...] = jnp.zeros((ROWS, 128), F32)
    lax.fori_loop(0, BLOCKS, student_block, 0)
    row_start(3, fold_lanes(row_wide[...]))
    col_finish(0)
    row_start(0, row_pass())
    student_turned[...] = student_unit[...].astype(F32).T.astype(BF16)

    def turn_block(block, carry):
        cols = columns(block)
        proto_turned[cols, :] = proto_unit[:, cols].T
        return carry

    lax.fori_loop(0, BLOCKS, turn_block, 0)
    student_total = row_finish(3)
    row_scale = 1.0 / (ALL_ROWS * row_finish(0))

    row_wide[...] = lane_broadcast(row_scale)
    col_pass()
    col_start(1)
    row_wide[...] = lane_broadcast((1.0 / STUDENT_TEMP) / student_total)

    def soft_rows(block, carry):
        rows = pl.ds(pl.multiple_of(block * 64, 64), 64)
        scale = row_wide[rows, :]
        for tile in range(TILES):
            cols = pl.ds(tile * 128, 128)
            soft_half[rows, cols] = (soft[rows, cols] * scale).astype(BF16)
        return carry

    lax.fori_loop(0, ROWS // 64, soft_rows, 0)
    unit_matmul(soft_half, pl.ds(0, ROWS))
    col_finish(1)
    row_start(1, row_pass())
    soft_x()
    row_scale = 1.0 / (ALL_ROWS * row_finish(1))

    row_wide[...] = lane_broadcast(row_scale)
    col_pass()
    col_start(2)
    soft_ring()
    soft_own = unit_own(0)
    col_finish(2)
    row_start(2, target_pass())
    unit_matmul(target_half, other)
    unit_x()
    unit_far(across, FAR)
    unit_matmul(target_half, mine)
    unit_send[1, mine, :] = unit_part[mine, :].astype(BF16)
    unit_far(here, 0)
    row_wide[...] = unit_part[:, :128] * student_unit[:, :128].astype(F32) + unit_part[:, 128:] * student_unit[
        :, 128:
    ].astype(F32)
    loss_row[0] = fold_lanes(row_wide[...])
    remote(loss_row.at[0], loss_pair, loss_sem.at[0], partner_x).start()
    unit_near()
    target_own = unit_own(1)
    landed(loss_pair, loss_sem.at[0])
    loss_row[1] = loss_row[0] + loss_pair[...]
    loss_recv[RING - 1] = loss_row[1]

    def loss_ring(step, carry):
        remote(
            loss_row.at[1], loss_recv.at[RING - 1 - step], loss_sem.at[1], (grp, here + z_peer(step))
        ).start()
        return carry

    lax.fori_loop(1, RING, loss_ring, 0)
    soft_unit = soft_finish(soft_own)
    row_scale = 1.0 / (ALL_ROWS * row_finish(2))
    row_wide[...] = lane_broadcast((ALL_ROWS / STUDENT_TEMP) * row_scale)

    def core_copy(block):
        return remote(core_send.at[block], core_recv.at[block], core_sem.at[block], partner_core)

    def term_ring(block):
        core_copy(block).wait()
        total = term_mine[block] + core_recv[block].astype(F32)
        term_mine[block] = total
        term_send[block] = total.astype(BF16)

        def send(step, carry):
            peer = chip_peer(step)
            remote(
                term_send.at[block, peer],
                term_recv.at[block, CHIPS - 1 - step],
                term_sem.at[block],
                (peer * 2 + core, proto),
            ).start()
            return carry

        lax.fori_loop(1, CHIPS, send, 0)

    def term_block(block, carry):
        cols = columns(block, TERM_BLOCK)
        scale = jnp.concatenate([row_wide[...]] * (TERM_BLOCK // 128), axis=1)
        dlogits = (soft_half[:, cols].astype(F32) - target_half[:, cols].astype(F32) * scale).astype(BF16)
        product = jnp.dot(student_turned[...], dlogits, preferred_element_type=F32)
        term[...] = product.reshape(CHIPS, 2, SHARE, TERM_BLOCK)
        core_send[block] = term[:, 1 - core].astype(BF16)
        core_copy(block).start()
        term_mine[block] = term[:, core]
        total = jnp.sum(product * proto_in[:, cols].astype(F32), axis=0, keepdims=True) * proto_scale[:, cols]
        for tile in range(TERM_BLOCK // 128):
            dots[pl.ds(block * (TERM_BLOCK // 128) + tile, 1), :] = total[:, tile * 128 : (tile + 1) * 128]

        @pl.when(block > 0)
        def _():
            term_ring(block - 1)

        return carry

    lax.fori_loop(0, TERM_BLOCKS, term_block, 0)
    term_ring(TERM_BLOCKS - 1)
    landed(loss_recv.at[pl.ds(0, RING - 1)], loss_sem.at[1])
    agreement = (ALL_ROWS / STUDENT_TEMP) * row_scale * ring_order(loss_recv)
    left(loss_pair, loss_sem.at[0])
    left(loss_recv.at[pl.ds(0, RING - 1)], loss_sem.at[1])
    loss_here = jnp.sum(jnp.log(student_total) - agreement) * (1.0 / ALL_ROWS)

    loss_send[...] = jnp.full((1, 128), loss_here, F32)
    loss_all[GRP - 1] = loss_send[...]
    dot_send[...] = dots[...].astype(BF16)
    dot_recv[GRP - 1] = dot_send[...]

    def dot_start(step, carry):
        device = (grp_peer(step), proto)
        remote(dot_send, dot_recv.at[GRP - 1 - step], dot_sem, device).start()
        remote(loss_send, loss_all.at[GRP - 1 - step], loss_sem.at[2], device).start()
        return carry

    lax.fori_loop(1, GRP, dot_start, 0)

    target_unit = unit_finish(target_own)
    my_rows = own_rows(here + z)
    unit_grad = soft_unit - target_unit * row_wide[my_rows, 0:1]
    wide, scaling = unit_rows(student_in[my_rows, :])
    row_dots = jnp.sum(wide * unit_grad, axis=1, keepdims=True)
    student_out[my_rows, :] = ((unit_grad - wide * row_dots) * scaling).astype(BF16)

    def out_send(step, base, sem):
        rows = student_out.at[my_rows]
        remote(rows, rows, sem, (grp, base + z_peer(step))).start()

    def out_far(step):
        out_send(step, across, out_sem.at[1])
        out_send(step, here, out_sem.at[1])

    def forward(owner):
        rows = student_out.at[own_rows(here + owner)]
        remote(rows, rows, out_sem.at[2], partner_x).start()

    far_steps(out_far)
    near_steps(lambda step: out_send(step, here, out_sem.at[0]))
    forward(z)

    near_out = student_out.at[pl.ds(0, 2 * NEAR * OWN)]
    landed(near_out, out_sem.at[0])
    near_steps(lambda step: forward(z_peer(step)))

    dot_arrivals = dot_recv.at[pl.ds(0, GRP - 1)]
    landed(dot_arrivals, dot_sem)
    total = dot_recv[0].astype(F32)
    for slot in range(1, GRP):
        total = total + dot_recv[slot].astype(F32)
    dots[...] = total
    left(dot_arrivals, dot_sem)
    loss_arrivals = loss_all.at[pl.ds(0, GRP - 1)]
    landed(loss_arrivals, loss_sem.at[2])
    total = jnp.zeros((1, 128), F32)
    for index in range(GRP):
        total = total + loss_all[lax.rem(index + GRP - 1 - grp + GRP, GRP)]
    loss_out[...] = total
    left(loss_arrivals, loss_sem.at[2])

    def term_finish(block, carry):
        cols = columns(block, TERM_BLOCK)

        arrivals = term_recv.at[block]
        landed(arrivals, term_sem.at[block])
        total = term_mine[block, chip]
        for slot in range(CHIPS - 1):
            total = total + term_recv[block, slot].astype(F32)
        left(arrivals, term_sem.at[block])
        scaling = proto_scale[:, cols]
        wide = proto_in[pl.ds(pl.multiple_of(grp * SHARE, SHARE), SHARE), cols].astype(F32) * scaling
        dot = jnp.concatenate(
            [dots[pl.ds(block * (TERM_BLOCK // 128) + tile, 1), :] for tile in range(TERM_BLOCK // 128)], axis=1
        )
        proto_out[:, cols] = ((total - wide * dot) * scaling).astype(BF16)
        return carry

    lax.fori_loop(0, TERM_BLOCKS, term_finish, 0)

    far_out = student_out.at[pl.ds(0, 2 * FAR * OWN)]
    passed_out = student_out.at[pl.ds(0, (2 * NEAR + 1) * OWN)]
    landed(far_out, out_sem.at[1])
    landed(passed_out, out_sem.at[2])
    left(near_out, out_sem.at[0])
    left(far_out, out_sem.at[1])
    left(passed_out, out_sem.at[2])


def per_device(teacher_features, student_features, prototypes):
    vmem = pltpu.VMEM
    dma = pltpu.SemaphoreType.DMA
    proto_grad, student_grad, loss = pl.pallas_call(
        kernel,
        out_shape=(
            vmem((SHARE, COLS), BF16),
            vmem((ROWS, WIDTH), BF16),
            jax.ShapeDtypeStruct((1, 128), F32),
        ),
        in_specs=[pl.BlockSpec(memory_space=pl.ANY)] * 3,
        out_specs=(pl.BlockSpec(memory_space=vmem),) * 3,
        scratch_shapes=[
            vmem((ROWS, WIDTH), BF16),
            vmem((ROWS, WIDTH), BF16),
            vmem((WIDTH, COLS), BF16),
            vmem((ROWS, WIDTH), BF16),
            vmem((WIDTH, ROWS), BF16),
            vmem((WIDTH, COLS), BF16),
            vmem((COLS, WIDTH), BF16),
            vmem((1, COLS), F32),
            vmem((ROWS, COLS), F32),
            vmem((ROWS, COLS), F32),
            vmem((ROWS, COLS), BF16),
            vmem((ROWS, COLS), BF16),
            vmem((ROWS, 128), F32),
            vmem((TILES, 128), F32),
            vmem((ITERS, TILES, 128), BF16),
            vmem((ITERS, GRP, TILES, 128), BF16),
            vmem((TILES, 128), F32),
            vmem((ITERS + 1, 4, 128), F32),
            vmem((ITERS + 1, 2 * RING, 4, 128), F32),
            vmem((2, 4, 128), F32),
            vmem((4, 128), F32),
            vmem((RING, 4, 128), F32),
            vmem((1, 128), F32),
            vmem((GRP, 1, 128), F32),
            vmem((ROWS, WIDTH), F32),
            vmem((2, ROWS, WIDTH), BF16),
            vmem((2, HALF_ROWS, WIDTH), BF16),
            vmem((2, HALF_ROWS, WIDTH), BF16),
            vmem((2, 2 * NEAR + 2 * FAR, OWN, WIDTH), BF16),
            vmem((CHIPS, 2, SHARE, TERM_BLOCK), F32),
            vmem((TERM_BLOCKS, CHIPS, SHARE, TERM_BLOCK), BF16),
            vmem((TERM_BLOCKS, CHIPS, SHARE, TERM_BLOCK), BF16),
            vmem((TERM_BLOCKS, CHIPS, SHARE, TERM_BLOCK), F32),
            vmem((TERM_BLOCKS, CHIPS, SHARE, TERM_BLOCK), BF16),
            vmem((TERM_BLOCKS, CHIPS - 1, SHARE, TERM_BLOCK), BF16),
            vmem((TILES, 128), F32),
            vmem((TILES, 128), BF16),
            vmem((GRP, TILES, 128), BF16),
            dma((2 + BLOCKS,)),
            dma((ITERS, 2)),
            dma((ITERS + 1, 2)),
            dma((3, 2)),
            dma((2, 2)),
            dma((2, 2)),
            dma((3, 2)),
            dma((TERM_BLOCKS, 2)),
            dma((TERM_BLOCKS, 2)),
            dma((2,)),
        ],
        compiler_params=pltpu.CompilerParams(
            collective_id=0, has_side_effects=True, vmem_limit_bytes=56 * 2**20
        ),
        name="sinkhorn_step",
    )(teacher_features, student_features, prototypes)
    return proto_grad, student_grad, loss[0, 0]


def solution(mesh):
    placed = (P("grp", None), P("grp", None), P(None, "proto"))
    return jax.shard_map(
        per_device,
        mesh=mesh,
        in_specs=placed,
        out_specs=(P("grp", "proto"), P("grp", None), P()),
        check_vma=False,
    )
```

```python
import functools
import math

import jax
import jax.numpy as jnp
from jax import lax
from jax.experimental import pallas as pl
from jax.experimental.pallas import tpu as pltpu
from jax.sharding import PartitionSpec as P

MESH = pl.DeviceIdType.MESH
F32 = jnp.float32
BF16 = jnp.bfloat16

ITERS = 3
TEACHER_TEMP = 0.07
STUDENT_TEMP = 0.1
EPSILON = 1e-06
LOG2E = math.log2(math.e)

ROWS = 512
COLS = 4096
WIDTH = 256
GRP = 16
RING = 16
ALL_ROWS = ROWS * GRP
ALL_COLS = COLS * 2 * RING
BLOCK = 512
BLOCKS = COLS // BLOCK
TILES = COLS // 128
TERM_BLOCK = 512
TERM_BLOCKS = COLS // TERM_BLOCK
HALF_ROWS = ROWS // 2
NEAR = 4
FAR = RING - 1 - 2 * NEAR
LAG = 3
SHARE = WIDTH // GRP
CHIPS = 8
OWN = ROWS // (2 * RING)


def lane_broadcast(vector):
    parts = []
    for group in range(4):
        parts.append(jnp.broadcast_to(vector[group : group + 1, :], (128, 128)).T)
    return jnp.concatenate(parts, axis=0)


def fold_lanes(partial):
    parts = []
    for group in range(4):
        block = partial[group * 128 : (group + 1) * 128, :].T
        parts.append(jnp.sum(block, axis=0, keepdims=True))
    return jnp.concatenate(parts, axis=0)


def kernel(
    teacher_hbm,
    student_hbm,
    proto_hbm,
    proto_out,
    student_out,
    loss_out,
    teacher_in,
    student_in,
    proto_in,
    student_unit,
    student_turned,
    proto_unit,
    proto_turned,
    proto_scale,
    exps,
    soft,
    soft_half,
    target_half,
    row_wide,
    col_sums,
    col_send,
    col_recv,
    col_scale,
    row_send,
    row_recv,
    loss_send,
    loss_proto,
    loss_all,
    unit_part,
    unit_send,
    unit_pair,
    unit_share,
    unit_recv,
    term,
    core_send,
    core_recv,
    term_mine,
    term_send,
    term_recv,
    dots,
    dot_send,
    dot_recv,
    in_sem,
    col_sem,
    row_sem,
    loss_sem,
    unit_x_sem,
    unit_z_sem,
    out_sem,
    core_sem,
    term_sem,
    dot_sem,
):
    grp = lax.axis_index("grp")
    proto = lax.axis_index("proto")
    core = lax.rem(grp, 2)
    chip = lax.div(grp, 2)
    x_lo = lax.div(proto, RING)
    z = lax.rem(proto, RING)
    partner_core = (grp + 1 - 2 * core, proto)
    partner_x = (grp, z + (1 - x_lo) * RING)
    here = x_lo * RING
    across = RING - here

    def grp_peer(step):
        return lax.rem(grp + step, GRP)

    def z_peer(step):
        return lax.rem(z + step, RING)

    def chip_peer(step):
        return lax.rem(chip + step, CHIPS)

    def near_steps(visit):
        def pair(step, carry):
            visit(NEAR + 1 - step)
            visit(RING - NEAR - 1 + step)
            return carry

        lax.fori_loop(1, NEAR + 1, pair, 0)

    def far_steps(visit):
        visit(RING // 2)

        def pair(step, carry):
            visit(RING // 2 - step)
            visit(RING // 2 + step)
            return carry

        lax.fori_loop(1, FAR // 2 + 1, pair, 0)

    def remote(src, dst, sem, device):
        return pltpu.make_async_remote_copy(
            src_ref=src,
            dst_ref=dst,
            send_sem=sem.at[0],
            recv_sem=sem.at[1],
            device_id=device,
            device_id_type=MESH,
        )

    def landed(ref, sem):
        remote(ref, ref, sem, partner_x).wait_recv()

    def left(ref, sem):
        remote(ref, ref, sem, partner_x).wait_send()

    loads = [
        pltpu.make_async_copy(teacher_hbm, teacher_in, in_sem.at[0]),
        pltpu.make_async_copy(student_hbm, student_in, in_sem.at[1]),
    ]

    def columns(block, size=BLOCK):
        return pl.ds(pl.multiple_of(block * size, size), size)

    def proto_load(block):
        cols = columns(block)
        return pltpu.make_async_copy(proto_hbm.at[:, cols], proto_in.at[:, cols], in_sem.at[2 + block])

    loads[0].start()
    lax.fori_loop(0, BLOCKS, lambda block, carry: (proto_load(block).start(), carry)[1], 0)
    loads[1].start()

    barrier = pltpu.get_barrier_semaphore()

    def greet_grp(step, carry):
        pl.semaphore_signal(barrier, inc=1, device_id=(grp_peer(step), proto), device_id_type=MESH)
        return carry

    def greet_proto(step, carry):
        pl.semaphore_signal(barrier, inc=1, device_id=(grp, lax.rem(proto + step, 2 * RING)), device_id_type=MESH)
        return carry

    lax.fori_loop(1, 2 * RING, greet_proto, 0)
    lax.fori_loop(1, GRP, greet_grp, 0)

    def unit_rows(features):
        wide = features.astype(F32)
        scaling = lax.rsqrt(jnp.sum(wide * wide, axis=1, keepdims=True) + EPSILON)
        return wide * scaling, scaling

    loads[0].wait()
    teacher_in[...] = unit_rows(teacher_in[...])[0].astype(BF16)

    def teacher_block(block, carry):
        proto_load(block).wait()
        cols = columns(block)
        wide = proto_in[:, cols].astype(F32)
        scaling = lax.rsqrt(jnp.sum(wide * wide, axis=0, keepdims=True) + EPSILON)
        proto_scale[:, cols] = scaling
        unit = (wide * scaling).astype(BF16)
        proto_unit[:, cols] = unit
        product = jnp.dot(teacher_in[...], unit, preferred_element_type=F32)
        values = jnp.exp2(product * (LOG2E / TEACHER_TEMP))
        exps[:, cols] = values
        total = jnp.sum(values, axis=0, keepdims=True)
        for tile in range(BLOCK // 128):
            col_sums[pl.ds(block * (BLOCK // 128) + tile, 1), :] = total[:, tile * 128 : (tile + 1) * 128]
        return carry

    lax.fori_loop(0, BLOCKS, teacher_block, 0)

    pl.semaphore_wait(barrier, GRP - 1 + 2 * RING - 1)

    def col_start(turn):
        message = col_sums[...].astype(BF16)
        col_send[turn] = message
        col_recv[turn, GRP - 1] = message

        def send(step, carry):
            remote(
                col_send.at[turn], col_recv.at[turn, GRP - 1 - step], col_sem.at[turn], (grp_peer(step), proto)
            ).start()
            return carry

        lax.fori_loop(1, GRP, send, 0)

    def col_finish(turn):
        arrivals = col_recv.at[turn, pl.ds(0, GRP - 1)]
        landed(arrivals, col_sem.at[turn])
        total = col_recv[turn, 0].astype(F32)
        for slot in range(1, GRP):
            total = total + col_recv[turn, slot].astype(F32)
        col_scale[...] = 1.0 / (ALL_COLS * total)
        left(arrivals, col_sem.at[turn])

    PEERS = 2 * RING - 1

    def spread(source, slots, sem):
        slots[PEERS] = source[...]

        def send(step, base, offset):
            remote(source, slots.at[PEERS - offset - step], sem, (grp, base + z_peer(step))).start()

        def four(step, carry):
            for base, offset in ((here, 0), (across, RING)):
                send(RING // 2 - step, base, offset)
                send(RING // 2 + step, base, offset)
            return carry

        send(RING // 2, across, RING)
        send(RING // 2, here, 0)
        lax.fori_loop(1, RING // 2, four, 0)
        send(0, across, RING)

    def gathered(slots, sem):
        arrivals = slots.at[pl.ds(0, PEERS)]
        landed(arrivals, sem)
        total = None
        for index in range(RING):
            slot = lax.rem(index + RING - 1 - z + RING, RING)
            pair = slots[RING + slot] + slots[slot]
            total = pair if total is None else total + pair
        left(arrivals, sem)
        return total

    def row_start(turn, sums):
        row_send[turn] = sums
        spread(row_send.at[turn], row_recv.at[turn], row_sem.at[turn])

    def row_finish(turn):
        return gathered(row_recv.at[turn], row_sem.at[turn])

    def row_pass():
        def rows_of(block, carry):
            rows = pl.ds(pl.multiple_of(block * 64, 64), 64)
            partial = jnp.zeros((64, 128), F32)
            for tile in range(TILES):
                partial = partial + exps[rows, pl.ds(tile * 128, 128)] * col_scale[pl.ds(tile, 1), :]
            row_wide[rows, :] = partial
            return carry

        lax.fori_loop(0, ROWS // 64, rows_of, 0)
        return fold_lanes(row_wide[...])

    def target_pass(first):
        def rows_of(block, carry):
            rows = pl.ds(pl.multiple_of(first + block * 64, 64), 64)
            partial = jnp.zeros((64, 128), F32)
            for tile in range(TILES):
                cols = pl.ds(tile * 128, 128)
                scaled = exps[rows, cols] * col_scale[pl.ds(tile, 1), :]
                target_half[rows, cols] = scaled.astype(BF16)
                partial = partial + scaled
            row_wide[rows, :] = partial
            return carry

        lax.fori_loop(0, HALF_ROWS // 64, rows_of, 0)

    def col_pass():
        def block_of(block, carry):
            cols = columns(block)
            partial = jnp.zeros((8, BLOCK), F32)
            for group in range(ROWS // 8):
                rows = pl.ds(group * 8, 8)
                scale = row_wide[rows, :]
                partial = partial + exps[rows, cols] * jnp.concatenate([scale] * (BLOCK // 128), axis=1)
            total = jnp.sum(partial, axis=0, keepdims=True)
            for tile in range(BLOCK // 128):
                col_sums[pl.ds(block * (BLOCK // 128) + tile, 1), :] = total[:, tile * 128 : (tile + 1) * 128]
            return carry

        lax.fori_loop(0, BLOCKS, block_of, 0)

    mine = pl.ds(pl.multiple_of(x_lo * HALF_ROWS, HALF_ROWS), HALF_ROWS)
    other = pl.ds(pl.multiple_of((1 - x_lo) * HALF_ROWS, HALF_ROWS), HALF_ROWS)

    def unit_matmul(source, rows):
        unit_part[rows, :] = jnp.dot(source[rows, :], proto_turned[...], preferred_element_type=F32)

    def own_rows(index):
        return pl.ds(pl.multiple_of(index * OWN, OWN), OWN)

    far_rows = pl.ds(0, FAR * OWN)
    near_rows = pl.ds(0, (2 * NEAR + 1) * OWN)

    def unit_x(part):
        unit_send[part] = unit_part[other, :].astype(BF16)

        def send(sem):
            def visit(step, carry):
                rows = own_rows(z_peer(step))
                remote(unit_send.at[part, rows], unit_pair.at[part, rows], sem, partner_x).start()
                return carry

            return visit

        lax.fori_loop(NEAR + 1, RING - NEAR, send(unit_x_sem.at[part, 0]), 0)
        lax.fori_loop(RING - NEAR, RING + NEAR + 1, send(unit_x_sem.at[part, 1]), 0)

    def unit_ring(part):
        def send(step):
            peer = z_peer(step)
            rows = own_rows(peer)
            total = unit_part[own_rows(here + peer), :] + unit_pair[part, rows, :].astype(F32)
            unit_share[part, rows, :] = total.astype(BF16)
            remote(
                unit_share.at[part, rows], unit_recv.at[part, step - 1], unit_z_sem.at[part], (grp, here + peer)
            ).start()

        landed(unit_pair.at[part, far_rows], unit_x_sem.at[part, 0])
        far_steps(send)
        landed(unit_pair.at[part, near_rows], unit_x_sem.at[part, 1])
        near_steps(send)
        return unit_part[own_rows(here + z), :] + unit_pair[part, own_rows(z), :].astype(F32)

    def unit_finish(part, total):
        landed(unit_recv.at[part], unit_z_sem.at[part])
        for slot in range(RING - 1):
            total = total + unit_recv[part, slot].astype(F32)
        left(unit_pair.at[part, far_rows], unit_x_sem.at[part, 0])
        left(unit_pair.at[part, near_rows], unit_x_sem.at[part, 1])
        left(unit_recv.at[part], unit_z_sem.at[part])
        return total

    col_start(0)
    loads[1].wait()
    student_unit[...] = unit_rows(student_in[...])[0].astype(BF16)

    def student_block(block, carry):
        cols = columns(block)
        product = jnp.dot(student_unit[...], proto_unit[:, cols], preferred_element_type=F32)
        values = jnp.exp2(product * (LOG2E / STUDENT_TEMP))
        soft[:, cols] = values
        partial = values[:, :128]
        for tile in range(1, BLOCK // 128):
            partial = partial + values[:, tile * 128 : (tile + 1) * 128]
        row_wide[...] = row_wide[...] + partial
        return carry

    row_wide[...] = jnp.zeros((ROWS, 128), F32)
    lax.fori_loop(0, BLOCKS, student_block, 0)
    row_start(3, fold_lanes(row_wide[...]))
    col_finish(0)
    row_start(0, row_pass())
    student_turned[...] = student_unit[...].astype(F32).T.astype(BF16)

    def turn_block(block, carry):
        cols = columns(block)
        proto_turned[cols, :] = proto_unit[:, cols].T
        return carry

    lax.fori_loop(0, BLOCKS, turn_block, 0)
    student_total = row_finish(3)
    row_scale = 1.0 / (ALL_ROWS * row_finish(0))

    row_wide[...] = lane_broadcast(row_scale)
    col_pass()
    col_start(1)
    row_wide[...] = lane_broadcast((1.0 / STUDENT_TEMP) / student_total)

    def soft_rows(block, carry):
        rows = pl.ds(pl.multiple_of(block * 64, 64), 64)
        scale = row_wide[rows, :]
        for tile in range(TILES):
            cols = pl.ds(tile * 128, 128)
            soft_half[rows, cols] = (soft[rows, cols] * scale).astype(BF16)
        return carry

    lax.fori_loop(0, ROWS // 64, soft_rows, 0)
    unit_matmul(soft_half, pl.ds(0, ROWS))
    col_finish(1)
    row_start(1, row_pass())
    unit_x(0)
    row_scale = 1.0 / (ALL_ROWS * row_finish(1))

    row_wide[...] = lane_broadcast(row_scale)
    col_pass()
    col_start(2)
    soft_own = unit_ring(0)
    col_finish(2)
    target_pass((1 - x_lo) * HALF_ROWS)
    unit_matmul(target_half, other)
    unit_x(1)
    target_pass(x_lo * HALF_ROWS)
    row_start(2, fold_lanes(row_wide[...]))
    unit_matmul(target_half, mine)
    target_own = unit_ring(1)
    row_wide[...] = unit_part[:, :128] * student_unit[:, :128].astype(F32) + unit_part[:, 128:] * student_unit[
        :, 128:
    ].astype(F32)
    agreement = fold_lanes(row_wide[...])
    soft_unit = unit_finish(0, soft_own)
    row_scale = 1.0 / (ALL_ROWS * row_finish(2))
    share = jnp.log(student_total) * (1.0 / (2 * RING)) - (ALL_ROWS / STUDENT_TEMP) * row_scale * agreement
    loss_send[0] = jnp.full((1, 128), jnp.sum(share) * (1.0 / ALL_ROWS), F32)
    spread(loss_send.at[0], loss_proto, loss_sem.at[0])
    row_wide[...] = lane_broadcast((ALL_ROWS / STUDENT_TEMP) * row_scale)

    def core_copy(block):
        return remote(core_send.at[block], core_recv.at[block], core_sem.at[block], partner_core)

    def term_ring(block):
        core_copy(block).wait()
        total = term_mine[block] + core_recv[block].astype(F32)
        term_mine[block] = total
        term_send[block] = total.astype(BF16)

        def send(step, carry):
            peer = chip_peer(step)
            remote(
                term_send.at[block, peer],
                term_recv.at[block, CHIPS - 1 - step],
                term_sem.at[block],
                (peer * 2 + core, proto),
            ).start()
            return carry

        lax.fori_loop(1, CHIPS, send, 0)

    def term_block(block, carry):
        cols = columns(block, TERM_BLOCK)
        scale = jnp.concatenate([row_wide[...]] * (TERM_BLOCK // 128), axis=1)
        dlogits = (soft_half[:, cols].astype(F32) - target_half[:, cols].astype(F32) * scale).astype(BF16)
        product = jnp.dot(student_turned[...], dlogits, preferred_element_type=F32)
        term[...] = product.reshape(CHIPS, 2, SHARE, TERM_BLOCK)
        core_send[block] = term[:, 1 - core].astype(BF16)
        core_copy(block).start()
        term_mine[block] = term[:, core]
        total = jnp.sum(product * proto_in[:, cols].astype(F32), axis=0, keepdims=True) * proto_scale[:, cols]
        for tile in range(TERM_BLOCK // 128):
            dots[pl.ds(block * (TERM_BLOCK // 128) + tile, 1), :] = total[:, tile * 128 : (tile + 1) * 128]

        @pl.when(block >= LAG)
        def _():
            term_ring(block - LAG)

        return carry

    lax.fori_loop(0, TERM_BLOCKS, term_block, 0)
    lax.fori_loop(TERM_BLOCKS - LAG, TERM_BLOCKS, lambda block, carry: (term_ring(block), carry)[1], 0)

    dot_send[...] = dots[...].astype(BF16)
    dot_recv[GRP - 1] = dot_send[...]

    def dot_start(step, carry):
        remote(dot_send, dot_recv.at[GRP - 1 - step], dot_sem, (grp_peer(step), proto)).start()
        return carry

    lax.fori_loop(1, GRP, dot_start, 0)

    target_unit = unit_finish(1, target_own)
    my_rows = own_rows(here + z)
    unit_grad = soft_unit - target_unit * row_wide[my_rows, 0:1]
    wide, scaling = unit_rows(student_in[my_rows, :])
    row_dots = jnp.sum(wide * unit_grad, axis=1, keepdims=True)
    student_out[my_rows, :] = ((unit_grad - wide * row_dots) * scaling).astype(BF16)

    def out_send(step, base, sem):
        rows = student_out.at[my_rows]
        remote(rows, rows, sem, (grp, base + z_peer(step))).start()

    def forward(owner):
        rows = student_out.at[own_rows(here + owner)]
        remote(rows, rows, out_sem.at[2], partner_x).start()

    far_steps(lambda step: out_send(step, here, out_sem.at[1]))
    near_steps(lambda step: out_send(step, here, out_sem.at[0]))
    forward(z)

    loss_send[1] = gathered(loss_proto, loss_sem.at[0])
    loss_all[GRP - 1] = loss_send[1]

    def loss_start(step, carry):
        remote(loss_send.at[1], loss_all.at[GRP - 1 - step], loss_sem.at[1], (grp_peer(step), proto)).start()
        return carry

    lax.fori_loop(1, GRP, loss_start, 0)

    near_out = student_out.at[pl.ds(0, 2 * NEAR * OWN)]
    far_out = student_out.at[pl.ds(0, FAR * OWN)]
    passed_out = student_out.at[pl.ds(0, RING * OWN)]
    landed(near_out, out_sem.at[0])
    near_steps(lambda step: forward(z_peer(step)))
    landed(far_out, out_sem.at[1])
    far_steps(lambda step: forward(z_peer(step)))

    dot_arrivals = dot_recv.at[pl.ds(0, GRP - 1)]
    landed(dot_arrivals, dot_sem)
    total = dot_recv[0].astype(F32)
    for slot in range(1, GRP):
        total = total + dot_recv[slot].astype(F32)
    dots[...] = total
    left(dot_arrivals, dot_sem)
    loss_arrivals = loss_all.at[pl.ds(0, GRP - 1)]
    landed(loss_arrivals, loss_sem.at[1])
    total = jnp.zeros((1, 128), F32)
    for index in range(GRP):
        total = total + loss_all[lax.rem(index + GRP - 1 - grp + GRP, GRP)]
    loss_out[...] = total
    left(loss_arrivals, loss_sem.at[1])

    def term_finish(block, carry):
        cols = columns(block, TERM_BLOCK)

        arrivals = term_recv.at[block]
        landed(arrivals, term_sem.at[block])
        total = term_mine[block, chip]
        for slot in range(CHIPS - 1):
            total = total + term_recv[block, slot].astype(F32)
        left(arrivals, term_sem.at[block])
        scaling = proto_scale[:, cols]
        wide = proto_in[pl.ds(pl.multiple_of(grp * SHARE, SHARE), SHARE), cols].astype(F32) * scaling
        dot = jnp.concatenate(
            [dots[pl.ds(block * (TERM_BLOCK // 128) + tile, 1), :] for tile in range(TERM_BLOCK // 128)], axis=1
        )
        proto_out[:, cols] = ((total - wide * dot) * scaling).astype(BF16)
        return carry

    lax.fori_loop(0, TERM_BLOCKS, term_finish, 0)

    landed(passed_out, out_sem.at[2])
    left(near_out, out_sem.at[0])
    left(far_out, out_sem.at[1])
    left(passed_out, out_sem.at[2])


def per_device(teacher_features, student_features, prototypes):
    vmem = pltpu.VMEM
    dma = pltpu.SemaphoreType.DMA
    proto_grad, student_grad, loss = pl.pallas_call(
        kernel,
        out_shape=(
            vmem((SHARE, COLS), BF16),
            vmem((ROWS, WIDTH), BF16),
            jax.ShapeDtypeStruct((1, 128), F32),
        ),
        in_specs=[pl.BlockSpec(memory_space=pl.ANY)] * 3,
        out_specs=(pl.BlockSpec(memory_space=vmem),) * 3,
        scratch_shapes=[
            vmem((ROWS, WIDTH), BF16),
            vmem((ROWS, WIDTH), BF16),
            vmem((WIDTH, COLS), BF16),
            vmem((ROWS, WIDTH), BF16),
            vmem((WIDTH, ROWS), BF16),
            vmem((WIDTH, COLS), BF16),
            vmem((COLS, WIDTH), BF16),
            vmem((1, COLS), F32),
            vmem((ROWS, COLS), F32),
            vmem((ROWS, COLS), F32),
            vmem((ROWS, COLS), BF16),
            vmem((ROWS, COLS), BF16),
            vmem((ROWS, 128), F32),
            vmem((TILES, 128), F32),
            vmem((ITERS, TILES, 128), BF16),
            vmem((ITERS, GRP, TILES, 128), BF16),
            vmem((TILES, 128), F32),
            vmem((ITERS + 1, 4, 128), F32),
            vmem((ITERS + 1, 2 * RING, 4, 128), F32),
            vmem((2, 1, 128), F32),
            vmem((2 * RING, 1, 128), F32),
            vmem((GRP, 1, 128), F32),
            vmem((ROWS, WIDTH), F32),
            vmem((2, HALF_ROWS, WIDTH), BF16),
            vmem((2, HALF_ROWS, WIDTH), BF16),
            vmem((2, HALF_ROWS, WIDTH), BF16),
            vmem((2, RING - 1, OWN, WIDTH), BF16),
            vmem((CHIPS, 2, SHARE, TERM_BLOCK), F32),
            vmem((TERM_BLOCKS, CHIPS, SHARE, TERM_BLOCK), BF16),
            vmem((TERM_BLOCKS, CHIPS, SHARE, TERM_BLOCK), BF16),
            vmem((TERM_BLOCKS, CHIPS, SHARE, TERM_BLOCK), F32),
            vmem((TERM_BLOCKS, CHIPS, SHARE, TERM_BLOCK), BF16),
            vmem((TERM_BLOCKS, CHIPS - 1, SHARE, TERM_BLOCK), BF16),
            vmem((TILES, 128), F32),
            vmem((TILES, 128), BF16),
            vmem((GRP, TILES, 128), BF16),
            dma((2 + BLOCKS,)),
            dma((ITERS, 2)),
            dma((ITERS + 1, 2)),
            dma((2, 2)),
            dma((2, 2, 2)),
            dma((2, 2)),
            dma((3, 2)),
            dma((TERM_BLOCKS, 2)),
            dma((TERM_BLOCKS, 2)),
            dma((2,)),
        ],
        compiler_params=pltpu.CompilerParams(
            collective_id=0, has_side_effects=True, vmem_limit_bytes=56 * 2**20
        ),
        name="sinkhorn_step",
    )(teacher_features, student_features, prototypes)
    return proto_grad, student_grad, loss[0, 0]


def solution(mesh):
    placed = (P("grp", None), P("grp", None), P(None, "proto"))
    return jax.shard_map(
        per_device,
        mesh=mesh,
        in_specs=placed,
        out_specs=(P("grp", "proto"), P("grp", None), P()),
        check_vma=False,
    )
```

```python
import functools
import math

import jax
import jax.numpy as jnp
from jax import lax
from jax.experimental import pallas as pl
from jax.experimental.pallas import tpu as pltpu
from jax.sharding import PartitionSpec as P

MESH = pl.DeviceIdType.MESH
F32 = jnp.float32
BF16 = jnp.bfloat16

ITERS = 3
TEACHER_TEMP = 0.07
STUDENT_TEMP = 0.1
EPSILON = 1e-06
LOG2E = math.log2(math.e)

ROWS = 512
COLS = 4096
WIDTH = 256
GRP = 16
RING = 16
ALL_ROWS = ROWS * GRP
ALL_COLS = COLS * 2 * RING
BLOCK = 512
BLOCKS = COLS // BLOCK
TILES = COLS // 128
TERM_BLOCK = 1024
TERM_BLOCKS = COLS // TERM_BLOCK
HALF_ROWS = ROWS // 2
NEAR = 4
FAR = RING - 1 - 2 * NEAR
LAG = 1
SHARE = WIDTH // GRP
CHIPS = 8
OWN = ROWS // (2 * RING)


def lane_broadcast(vector):
    parts = []
    for group in range(4):
        parts.append(jnp.broadcast_to(vector[group : group + 1, :], (128, 128)).T)
    return jnp.concatenate(parts, axis=0)


def fold_lanes(partial):
    parts = []
    for group in range(4):
        block = partial[group * 128 : (group + 1) * 128, :].T
        parts.append(jnp.sum(block, axis=0, keepdims=True))
    return jnp.concatenate(parts, axis=0)


def kernel(
    teacher_hbm,
    student_hbm,
    proto_hbm,
    proto_out,
    student_out,
    loss_out,
    teacher_in,
    student_in,
    proto_in,
    student_unit,
    student_turned,
    proto_unit,
    proto_turned,
    proto_scale,
    exps,
    soft,
    soft_half,
    target_half,
    row_wide,
    col_sums,
    col_send,
    col_recv,
    col_scale,
    row_send,
    row_recv,
    loss_send,
    loss_proto,
    loss_all,
    unit_part,
    unit_send,
    unit_pair,
    unit_share,
    unit_recv,
    term,
    core_send,
    core_recv,
    term_mine,
    term_send,
    term_recv,
    dots,
    dot_send,
    dot_recv,
    in_sem,
    col_sem,
    row_sem,
    loss_sem,
    unit_x_sem,
    unit_z_sem,
    out_sem,
    core_sem,
    term_sem,
    dot_sem,
):
    grp = lax.axis_index("grp")
    proto = lax.axis_index("proto")
    core = lax.rem(grp, 2)
    chip = lax.div(grp, 2)
    x_lo = lax.div(proto, RING)
    z = lax.rem(proto, RING)
    partner_core = (grp + 1 - 2 * core, proto)
    partner_x = (grp, z + (1 - x_lo) * RING)
    here = x_lo * RING
    across = RING - here

    def grp_peer(step):
        return lax.rem(grp + step, GRP)

    def z_peer(step):
        return lax.rem(z + step, RING)

    def chip_peer(step):
        return lax.rem(chip + step, CHIPS)

    def near_steps(visit):
        def pair(step, carry):
            visit(NEAR + 1 - step)
            visit(RING - NEAR - 1 + step)
            return carry

        lax.fori_loop(1, NEAR + 1, pair, 0)

    def far_steps(visit):
        visit(RING // 2)

        def pair(step, carry):
            visit(RING // 2 - step)
            visit(RING // 2 + step)
            return carry

        lax.fori_loop(1, FAR // 2 + 1, pair, 0)

    def remote(src, dst, sem, device):
        return pltpu.make_async_remote_copy(
            src_ref=src,
            dst_ref=dst,
            send_sem=sem.at[0],
            recv_sem=sem.at[1],
            device_id=device,
            device_id_type=MESH,
        )

    def landed(ref, sem):
        remote(ref, ref, sem, partner_x).wait_recv()

    def left(ref, sem):
        remote(ref, ref, sem, partner_x).wait_send()

    loads = [
        pltpu.make_async_copy(teacher_hbm, teacher_in, in_sem.at[0]),
        pltpu.make_async_copy(student_hbm, student_in, in_sem.at[1]),
    ]

    def columns(block, size=BLOCK):
        return pl.ds(pl.multiple_of(block * size, size), size)

    def proto_load(block):
        cols = columns(block)
        return pltpu.make_async_copy(proto_hbm.at[:, cols], proto_in.at[:, cols], in_sem.at[2 + block])

    loads[0].start()
    lax.fori_loop(0, BLOCKS, lambda block, carry: (proto_load(block).start(), carry)[1], 0)
    loads[1].start()

    barrier = pltpu.get_barrier_semaphore()

    def greet_grp(step, carry):
        pl.semaphore_signal(barrier, inc=1, device_id=(grp_peer(step), proto), device_id_type=MESH)
        return carry

    def greet_proto(step, carry):
        pl.semaphore_signal(barrier, inc=1, device_id=(grp, lax.rem(proto + step, 2 * RING)), device_id_type=MESH)
        return carry

    lax.fori_loop(1, 2 * RING, greet_proto, 0)
    lax.fori_loop(1, GRP, greet_grp, 0)

    def unit_rows(features):
        wide = features.astype(F32)
        scaling = lax.rsqrt(jnp.sum(wide * wide, axis=1, keepdims=True) + EPSILON)
        return wide * scaling, scaling

    loads[0].wait()
    teacher_in[...] = unit_rows(teacher_in[...])[0].astype(BF16)

    def teacher_block(block, carry):
        proto_load(block).wait()
        cols = columns(block)
        wide = proto_in[:, cols].astype(F32)
        scaling = lax.rsqrt(jnp.sum(wide * wide, axis=0, keepdims=True) + EPSILON)
        proto_scale[:, cols] = scaling
        unit = (wide * scaling).astype(BF16)
        proto_unit[:, cols] = unit
        product = jnp.dot(teacher_in[...], unit, preferred_element_type=F32)
        values = jnp.exp2(product * (LOG2E / TEACHER_TEMP))
        exps[:, cols] = values
        total = jnp.sum(values, axis=0, keepdims=True)
        for tile in range(BLOCK // 128):
            col_sums[pl.ds(block * (BLOCK // 128) + tile, 1), :] = total[:, tile * 128 : (tile + 1) * 128]
        return carry

    lax.fori_loop(0, BLOCKS, teacher_block, 0)

    pl.semaphore_wait(barrier, GRP - 1 + 2 * RING - 1)

    def col_start(turn):
        message = col_sums[...].astype(BF16)
        col_send[turn] = message
        col_recv[turn, GRP - 1] = message

        def send(step, carry):
            remote(
                col_send.at[turn], col_recv.at[turn, GRP - 1 - step], col_sem.at[turn], (grp_peer(step), proto)
            ).start()
            return carry

        lax.fori_loop(1, GRP, send, 0)

    def col_finish(turn):
        arrivals = col_recv.at[turn, pl.ds(0, GRP - 1)]
        landed(arrivals, col_sem.at[turn])
        total = col_recv[turn, 0].astype(F32)
        for slot in range(1, GRP):
            total = total + col_recv[turn, slot].astype(F32)
        col_scale[...] = 1.0 / (ALL_COLS * total)
        left(arrivals, col_sem.at[turn])

    PEERS = 2 * RING - 1

    def spread(source, slots, sem):
        slots[PEERS] = source[...]

        def send(step, base, offset):
            remote(source, slots.at[PEERS - offset - step], sem, (grp, base + z_peer(step))).start()

        def four(step, carry):
            for base, offset in ((here, 0), (across, RING)):
                send(RING // 2 - step, base, offset)
                send(RING // 2 + step, base, offset)
            return carry

        send(RING // 2, across, RING)
        send(RING // 2, here, 0)
        lax.fori_loop(1, RING // 2, four, 0)
        send(0, across, RING)

    def gathered(slots, sem):
        arrivals = slots.at[pl.ds(0, PEERS)]
        landed(arrivals, sem)
        total = None
        for index in range(RING):
            slot = lax.rem(index + RING - 1 - z + RING, RING)
            pair = slots[RING + slot] + slots[slot]
            total = pair if total is None else total + pair
        left(arrivals, sem)
        return total

    def row_start(turn, sums):
        row_send[turn] = sums
        spread(row_send.at[turn], row_recv.at[turn], row_sem.at[turn])

    def row_finish(turn):
        return gathered(row_recv.at[turn], row_sem.at[turn])

    def row_pass():
        def rows_of(block, carry):
            rows = pl.ds(pl.multiple_of(block * 64, 64), 64)
            partial = jnp.zeros((64, 128), F32)
            for tile in range(TILES):
                partial = partial + exps[rows, pl.ds(tile * 128, 128)] * col_scale[pl.ds(tile, 1), :]
            row_wide[rows, :] = partial
            return carry

        lax.fori_loop(0, ROWS // 64, rows_of, 0)
        return fold_lanes(row_wide[...])

    def target_pass():
        def rows_of(block, carry):
            rows = pl.ds(pl.multiple_of(block * 64, 64), 64)
            partial = jnp.zeros((64, 128), F32)
            for tile in range(TILES):
                cols = pl.ds(tile * 128, 128)
                scaled = exps[rows, cols] * col_scale[pl.ds(tile, 1), :]
                target_half[rows, cols] = scaled.astype(BF16)
                partial = partial + scaled
            row_wide[rows, :] = partial
            return carry

        lax.fori_loop(0, ROWS // 64, rows_of, 0)

    def col_pass():
        def block_of(block, carry):
            cols = columns(block)
            partial = jnp.zeros((8, BLOCK), F32)
            for group in range(ROWS // 8):
                rows = pl.ds(group * 8, 8)
                scale = row_wide[rows, :]
                partial = partial + exps[rows, cols] * jnp.concatenate([scale] * (BLOCK // 128), axis=1)
            total = jnp.sum(partial, axis=0, keepdims=True)
            for tile in range(BLOCK // 128):
                col_sums[pl.ds(block * (BLOCK // 128) + tile, 1), :] = total[:, tile * 128 : (tile + 1) * 128]
            return carry

        lax.fori_loop(0, BLOCKS, block_of, 0)

    mine = pl.ds(pl.multiple_of(x_lo * HALF_ROWS, HALF_ROWS), HALF_ROWS)
    other = pl.ds(pl.multiple_of((1 - x_lo) * HALF_ROWS, HALF_ROWS), HALF_ROWS)

    def unit_matmul(source, rows):
        unit_part[rows, :] = jnp.dot(source[rows, :], proto_turned[...], preferred_element_type=F32)

    def own_rows(index):
        return pl.ds(pl.multiple_of(index * OWN, OWN), OWN)

    far_rows = pl.ds(0, FAR * OWN)
    near_rows = pl.ds(0, (2 * NEAR + 1) * OWN)

    def unit_x(part):
        unit_send[part] = unit_part[other, :].astype(BF16)

        def send(sem):
            def visit(step, carry):
                rows = own_rows(z_peer(step))
                remote(unit_send.at[part, rows], unit_pair.at[part, rows], sem, partner_x).start()
                return carry

            return visit

        lax.fori_loop(NEAR + 1, RING - NEAR, send(unit_x_sem.at[part, 0]), 0)
        lax.fori_loop(RING - NEAR, RING + NEAR + 1, send(unit_x_sem.at[part, 1]), 0)

    def unit_ring(part):
        def send(step):
            peer = z_peer(step)
            rows = own_rows(peer)
            total = unit_part[own_rows(here + peer), :] + unit_pair[part, rows, :].astype(F32)
            unit_share[part, rows, :] = total.astype(BF16)
            remote(
                unit_share.at[part, rows], unit_recv.at[part, step - 1], unit_z_sem.at[part], (grp, here + peer)
            ).start()

        landed(unit_pair.at[part, far_rows], unit_x_sem.at[part, 0])
        far_steps(send)
        landed(unit_pair.at[part, near_rows], unit_x_sem.at[part, 1])
        near_steps(send)
        return unit_part[own_rows(here + z), :] + unit_pair[part, own_rows(z), :].astype(F32)

    def unit_finish(part, total):
        landed(unit_recv.at[part], unit_z_sem.at[part])
        for slot in range(RING - 1):
            total = total + unit_recv[part, slot].astype(F32)
        left(unit_pair.at[part, far_rows], unit_x_sem.at[part, 0])
        left(unit_pair.at[part, near_rows], unit_x_sem.at[part, 1])
        left(unit_recv.at[part], unit_z_sem.at[part])
        return total

    col_start(0)
    loads[1].wait()
    student_unit[...] = unit_rows(student_in[...])[0].astype(BF16)

    def student_block(block, carry):
        cols = columns(block)
        product = jnp.dot(student_unit[...], proto_unit[:, cols], preferred_element_type=F32)
        values = jnp.exp2(product * (LOG2E / STUDENT_TEMP))
        soft[:, cols] = values
        partial = values[:, :128]
        for tile in range(1, BLOCK // 128):
            partial = partial + values[:, tile * 128 : (tile + 1) * 128]
        row_wide[...] = row_wide[...] + partial
        return carry

    row_wide[...] = jnp.zeros((ROWS, 128), F32)
    lax.fori_loop(0, BLOCKS, student_block, 0)
    row_start(3, fold_lanes(row_wide[...]))
    col_finish(0)
    row_start(0, row_pass())
    student_turned[...] = student_unit[...].astype(F32).T.astype(BF16)

    def turn_block(block, carry):
        cols = columns(block)
        proto_turned[cols, :] = proto_unit[:, cols].T
        return carry

    lax.fori_loop(0, BLOCKS, turn_block, 0)
    student_total = row_finish(3)
    row_scale = 1.0 / (ALL_ROWS * row_finish(0))

    row_wide[...] = lane_broadcast(row_scale)
    col_pass()
    col_start(1)
    row_wide[...] = lane_broadcast((1.0 / STUDENT_TEMP) / student_total)

    def soft_rows(block, carry):
        rows = pl.ds(pl.multiple_of(block * 64, 64), 64)
        scale = row_wide[rows, :]
        for tile in range(TILES):
            cols = pl.ds(tile * 128, 128)
            soft_half[rows, cols] = (soft[rows, cols] * scale).astype(BF16)
        return carry

    lax.fori_loop(0, ROWS // 64, soft_rows, 0)
    unit_matmul(soft_half, pl.ds(0, ROWS))
    unit_x(0)
    col_finish(1)
    row_start(1, row_pass())
    row_scale = 1.0 / (ALL_ROWS * row_finish(1))

    row_wide[...] = lane_broadcast(row_scale)
    col_pass()
    col_start(2)
    soft_own = unit_ring(0)
    col_finish(2)
    target_pass()
    row_start(2, fold_lanes(row_wide[...]))
    unit_matmul(target_half, other)
    unit_x(1)
    unit_matmul(target_half, mine)
    target_own = unit_ring(1)
    row_wide[...] = unit_part[:, :128] * student_unit[:, :128].astype(F32) + unit_part[:, 128:] * student_unit[
        :, 128:
    ].astype(F32)
    agreement = fold_lanes(row_wide[...])
    soft_unit = unit_finish(0, soft_own)
    row_scale = 1.0 / (ALL_ROWS * row_finish(2))
    share = jnp.log(student_total) * (1.0 / (2 * RING)) - (ALL_ROWS / STUDENT_TEMP) * row_scale * agreement
    loss_send[0] = jnp.full((1, 128), jnp.sum(share) * (1.0 / ALL_ROWS), F32)
    spread(loss_send.at[0], loss_proto, loss_sem.at[0])
    row_wide[...] = lane_broadcast((ALL_ROWS / STUDENT_TEMP) * row_scale)

    def core_copy(block):
        return remote(core_send.at[block], core_recv.at[block], core_sem.at[block], partner_core)

    def term_ring(block):
        core_copy(block).wait()
        total = term_mine[block] + core_recv[block].astype(F32)
        term_mine[block] = total
        term_send[block] = total.astype(BF16)

        def send(step, carry):
            peer = chip_peer(step)
            remote(
                term_send.at[block, peer],
                term_recv.at[block, CHIPS - 1 - step],
                term_sem.at[block],
                (peer * 2 + core, proto),
            ).start()
            return carry

        lax.fori_loop(1, CHIPS, send, 0)

    def term_block(block, carry):
        cols = columns(block, TERM_BLOCK)
        scale = jnp.concatenate([row_wide[...]] * (TERM_BLOCK // 128), axis=1)
        dlogits = (soft_half[:, cols].astype(F32) - target_half[:, cols].astype(F32) * scale).astype(BF16)
        product = jnp.dot(student_turned[...], dlogits, preferred_element_type=F32)
        term[...] = product.reshape(CHIPS, 2, SHARE, TERM_BLOCK)
        core_send[block] = term[:, 1 - core].astype(BF16)
        core_copy(block).start()
        term_mine[block] = term[:, core]
        total = jnp.sum(product * proto_in[:, cols].astype(F32), axis=0, keepdims=True) * proto_scale[:, cols]
        for tile in range(TERM_BLOCK // 128):
            dots[pl.ds(block * (TERM_BLOCK // 128) + tile, 1), :] = total[:, tile * 128 : (tile + 1) * 128]

        @pl.when(block >= LAG)
        def _():
            term_ring(block - LAG)

        return carry

    lax.fori_loop(0, TERM_BLOCKS, term_block, 0)
    lax.fori_loop(TERM_BLOCKS - LAG, TERM_BLOCKS, lambda block, carry: (term_ring(block), carry)[1], 0)

    dot_send[...] = dots[...].astype(BF16)
    dot_recv[GRP - 1] = dot_send[...]

    def dot_start(step, carry):
        remote(dot_send, dot_recv.at[GRP - 1 - step], dot_sem, (grp_peer(step), proto)).start()
        return carry

    lax.fori_loop(1, GRP, dot_start, 0)

    target_unit = unit_finish(1, target_own)
    my_rows = own_rows(here + z)
    unit_grad = soft_unit - target_unit * row_wide[my_rows, 0:1]
    wide, scaling = unit_rows(student_in[my_rows, :])
    row_dots = jnp.sum(wide * unit_grad, axis=1, keepdims=True)
    student_out[my_rows, :] = ((unit_grad - wide * row_dots) * scaling).astype(BF16)

    def out_send(step, base, sem):
        rows = student_out.at[my_rows]
        remote(rows, rows, sem, (grp, base + z_peer(step))).start()

    def forward(owner):
        rows = student_out.at[own_rows(here + owner)]
        remote(rows, rows, out_sem.at[2], partner_x).start()

    far_steps(lambda step: out_send(step, here, out_sem.at[1]))
    near_steps(lambda step: out_send(step, here, out_sem.at[0]))
    forward(z)

    loss_send[1] = gathered(loss_proto, loss_sem.at[0])
    loss_all[GRP - 1] = loss_send[1]

    def loss_start(step, carry):
        remote(loss_send.at[1], loss_all.at[GRP - 1 - step], loss_sem.at[1], (grp_peer(step), proto)).start()
        return carry

    lax.fori_loop(1, GRP, loss_start, 0)

    near_out = student_out.at[pl.ds(0, 2 * NEAR * OWN)]
    far_out = student_out.at[pl.ds(0, FAR * OWN)]
    passed_out = student_out.at[pl.ds(0, RING * OWN)]
    landed(near_out, out_sem.at[0])
    near_steps(lambda step: forward(z_peer(step)))
    landed(far_out, out_sem.at[1])
    far_steps(lambda step: forward(z_peer(step)))

    dot_arrivals = dot_recv.at[pl.ds(0, GRP - 1)]
    landed(dot_arrivals, dot_sem)
    total = dot_recv[0].astype(F32)
    for slot in range(1, GRP):
        total = total + dot_recv[slot].astype(F32)
    dots[...] = total
    left(dot_arrivals, dot_sem)
    loss_arrivals = loss_all.at[pl.ds(0, GRP - 1)]
    landed(loss_arrivals, loss_sem.at[1])
    total = jnp.zeros((1, 128), F32)
    for index in range(GRP):
        total = total + loss_all[lax.rem(index + GRP - 1 - grp + GRP, GRP)]
    loss_out[...] = total
    left(loss_arrivals, loss_sem.at[1])

    def term_finish(block, carry):
        cols = columns(block, TERM_BLOCK)

        arrivals = term_recv.at[block]
        landed(arrivals, term_sem.at[block])
        total = term_mine[block, chip]
        for slot in range(CHIPS - 1):
            total = total + term_recv[block, slot].astype(F32)
        left(arrivals, term_sem.at[block])
        scaling = proto_scale[:, cols]
        wide = proto_in[pl.ds(pl.multiple_of(grp * SHARE, SHARE), SHARE), cols].astype(F32) * scaling
        dot = jnp.concatenate(
            [dots[pl.ds(block * (TERM_BLOCK // 128) + tile, 1), :] for tile in range(TERM_BLOCK // 128)], axis=1
        )
        proto_out[:, cols] = ((total - wide * dot) * scaling).astype(BF16)
        return carry

    lax.fori_loop(0, TERM_BLOCKS, term_finish, 0)

    landed(passed_out, out_sem.at[2])
    left(near_out, out_sem.at[0])
    left(far_out, out_sem.at[1])
    left(passed_out, out_sem.at[2])


def per_device(teacher_features, student_features, prototypes):
    vmem = pltpu.VMEM
    dma = pltpu.SemaphoreType.DMA
    proto_grad, student_grad, loss = pl.pallas_call(
        kernel,
        out_shape=(
            vmem((SHARE, COLS), BF16),
            vmem((ROWS, WIDTH), BF16),
            jax.ShapeDtypeStruct((1, 128), F32),
        ),
        in_specs=[pl.BlockSpec(memory_space=pl.ANY)] * 3,
        out_specs=(pl.BlockSpec(memory_space=vmem),) * 3,
        scratch_shapes=[
            vmem((ROWS, WIDTH), BF16),
            vmem((ROWS, WIDTH), BF16),
            vmem((WIDTH, COLS), BF16),
            vmem((ROWS, WIDTH), BF16),
            vmem((WIDTH, ROWS), BF16),
            vmem((WIDTH, COLS), BF16),
            vmem((COLS, WIDTH), BF16),
            vmem((1, COLS), F32),
            vmem((ROWS, COLS), F32),
            vmem((ROWS, COLS), F32),
            vmem((ROWS, COLS), BF16),
            vmem((ROWS, COLS), BF16),
            vmem((ROWS, 128), F32),
            vmem((TILES, 128), F32),
            vmem((ITERS, TILES, 128), BF16),
            vmem((ITERS, GRP, TILES, 128), BF16),
            vmem((TILES, 128), F32),
            vmem((ITERS + 1, 4, 128), F32),
            vmem((ITERS + 1, 2 * RING, 4, 128), F32),
            vmem((2, 1, 128), F32),
            vmem((2 * RING, 1, 128), F32),
            vmem((GRP, 1, 128), F32),
            vmem((ROWS, WIDTH), F32),
            vmem((2, HALF_ROWS, WIDTH), BF16),
            vmem((2, HALF_ROWS, WIDTH), BF16),
            vmem((2, HALF_ROWS, WIDTH), BF16),
            vmem((2, RING - 1, OWN, WIDTH), BF16),
            vmem((CHIPS, 2, SHARE, TERM_BLOCK), F32),
            vmem((TERM_BLOCKS, CHIPS, SHARE, TERM_BLOCK), BF16),
            vmem((TERM_BLOCKS, CHIPS, SHARE, TERM_BLOCK), BF16),
            vmem((TERM_BLOCKS, CHIPS, SHARE, TERM_BLOCK), F32),
            vmem((TERM_BLOCKS, CHIPS, SHARE, TERM_BLOCK), BF16),
            vmem((TERM_BLOCKS, CHIPS - 1, SHARE, TERM_BLOCK), BF16),
            vmem((TILES, 128), F32),
            vmem((TILES, 128), BF16),
            vmem((GRP, TILES, 128), BF16),
            dma((2 + BLOCKS,)),
            dma((ITERS, 2)),
            dma((ITERS + 1, 2)),
            dma((2, 2)),
            dma((2, 2, 2)),
            dma((2, 2)),
            dma((3, 2)),
            dma((TERM_BLOCKS, 2)),
            dma((TERM_BLOCKS, 2)),
            dma((2,)),
        ],
        compiler_params=pltpu.CompilerParams(
            collective_id=0, has_side_effects=True, vmem_limit_bytes=56 * 2**20
        ),
        name="sinkhorn_step",
    )(teacher_features, student_features, prototypes)
    return proto_grad, student_grad, loss[0, 0]


def solution(mesh):
    placed = (P("grp", None), P("grp", None), P(None, "proto"))
    return jax.shard_map(
        per_device,
        mesh=mesh,
        in_specs=placed,
        out_specs=(P("grp", "proto"), P("grp", None), P()),
        check_vma=False,
    )
```

```python
import functools
import math

import jax
import jax.numpy as jnp
from jax import lax
from jax.experimental import pallas as pl
from jax.experimental.pallas import tpu as pltpu
from jax.sharding import PartitionSpec as P

MESH = pl.DeviceIdType.MESH
F32 = jnp.float32
BF16 = jnp.bfloat16

ITERS = 3
TEACHER_TEMP = 0.07
STUDENT_TEMP = 0.1
EPSILON = 1e-06
LOG2E = math.log2(math.e)

ROWS = 512
COLS = 4096
WIDTH = 256
GRP = 16
RING = 16
ALL_ROWS = ROWS * GRP
ALL_COLS = COLS * 2 * RING
BLOCK = 512
BLOCKS = COLS // BLOCK
TILES = COLS // 128
TERM_BLOCK = 1024
TERM_BLOCKS = COLS // TERM_BLOCK
HALF_ROWS = ROWS // 2
NEAR = 4
FAR = RING - 1 - 2 * NEAR
GRP_STEPS = (6, 10, 7, 9, 2, 14, 5, 11, 8, 3, 13, 1, 15, 4, 12)
CHIP_STEPS = (3, 5, 1, 7, 4, 2, 6)
LAG = 2
SHARE = WIDTH // GRP
CHIPS = 8
OWN = ROWS // (2 * RING)


def lane_broadcast(vector):
    parts = []
    for group in range(4):
        parts.append(jnp.broadcast_to(vector[group : group + 1, :], (128, 128)).T)
    return jnp.concatenate(parts, axis=0)


def fold_lanes(partial):
    parts = []
    for group in range(4):
        block = partial[group * 128 : (group + 1) * 128, :].T
        parts.append(jnp.sum(block, axis=0, keepdims=True))
    return jnp.concatenate(parts, axis=0)


def kernel(
    teacher_hbm,
    student_hbm,
    proto_hbm,
    proto_out,
    student_out,
    loss_out,
    teacher_in,
    student_in,
    proto_in,
    student_unit,
    student_turned,
    proto_unit,
    proto_turned,
    proto_scale,
    exps,
    soft,
    soft_half,
    target_half,
    row_wide,
    col_sums,
    col_send,
    col_recv,
    col_scale,
    row_send,
    row_recv,
    loss_send,
    loss_proto,
    loss_all,
    unit_part,
    unit_send,
    unit_pair,
    unit_share,
    unit_recv,
    term,
    core_send,
    core_recv,
    term_mine,
    term_send,
    term_recv,
    dots,
    dot_send,
    dot_recv,
    in_sem,
    col_sem,
    row_sem,
    loss_sem,
    unit_x_sem,
    unit_z_sem,
    out_sem,
    core_sem,
    term_sem,
    dot_sem,
):
    grp = lax.axis_index("grp")
    proto = lax.axis_index("proto")
    core = lax.rem(grp, 2)
    chip = lax.div(grp, 2)
    x_lo = lax.div(proto, RING)
    z = lax.rem(proto, RING)
    partner_core = (grp + 1 - 2 * core, proto)
    partner_x = (grp, z + (1 - x_lo) * RING)
    here = x_lo * RING
    across = RING - here

    def grp_peer(step):
        return lax.rem(grp + step, GRP)

    def z_peer(step):
        return lax.rem(z + step, RING)

    def chip_peer(step):
        return lax.rem(chip + step, CHIPS)

    def near_steps(visit):
        def pair(step, carry):
            visit(NEAR + 1 - step)
            visit(RING - NEAR - 1 + step)
            return carry

        lax.fori_loop(1, NEAR + 1, pair, 0)

    def far_steps(visit):
        visit(RING // 2)

        def pair(step, carry):
            visit(RING // 2 - step)
            visit(RING // 2 + step)
            return carry

        lax.fori_loop(1, FAR // 2 + 1, pair, 0)

    def remote(src, dst, sem, device):
        return pltpu.make_async_remote_copy(
            src_ref=src,
            dst_ref=dst,
            send_sem=sem.at[0],
            recv_sem=sem.at[1],
            device_id=device,
            device_id_type=MESH,
        )

    def landed(ref, sem):
        remote(ref, ref, sem, partner_x).wait_recv()

    def left(ref, sem):
        remote(ref, ref, sem, partner_x).wait_send()

    loads = [
        pltpu.make_async_copy(teacher_hbm, teacher_in, in_sem.at[0]),
        pltpu.make_async_copy(student_hbm, student_in, in_sem.at[1]),
    ]

    def columns(block, size=BLOCK):
        return pl.ds(pl.multiple_of(block * size, size), size)

    def proto_load(block):
        cols = columns(block)
        return pltpu.make_async_copy(proto_hbm.at[:, cols], proto_in.at[:, cols], in_sem.at[2 + block])

    loads[0].start()
    lax.fori_loop(0, BLOCKS, lambda block, carry: (proto_load(block).start(), carry)[1], 0)
    loads[1].start()

    barrier = pltpu.get_barrier_semaphore()

    def greet_grp(step, carry):
        pl.semaphore_signal(barrier, inc=1, device_id=(grp_peer(step), proto), device_id_type=MESH)
        return carry

    def greet_proto(step, carry):
        pl.semaphore_signal(barrier, inc=1, device_id=(grp, lax.rem(proto + step, 2 * RING)), device_id_type=MESH)
        return carry

    lax.fori_loop(1, 2 * RING, greet_proto, 0)
    lax.fori_loop(1, GRP, greet_grp, 0)

    def unit_rows(features):
        wide = features.astype(F32)
        scaling = lax.rsqrt(jnp.sum(wide * wide, axis=1, keepdims=True) + EPSILON)
        return wide * scaling, scaling

    def unit_all(features):
        wide = features.astype(F32)
        squares = wide * wide
        high = squares.astype(BF16)
        low = (squares - high.astype(F32)).astype(BF16)
        ones = jnp.ones((WIDTH, 128), BF16)
        total = jnp.dot(high, ones, preferred_element_type=F32) + jnp.dot(low, ones, preferred_element_type=F32)
        scaling = lax.rsqrt(total + EPSILON)
        return (wide * jnp.concatenate([scaling] * (WIDTH // 128), axis=1)).astype(BF16)

    loads[0].wait()
    teacher_in[...] = unit_all(teacher_in[...])

    def teacher_block(block, carry):
        proto_load(block).wait()
        cols = columns(block)
        wide = proto_in[:, cols].astype(F32)
        scaling = lax.rsqrt(jnp.sum(wide * wide, axis=0, keepdims=True) + EPSILON)
        proto_scale[:, cols] = scaling
        unit = (wide * scaling).astype(BF16)
        proto_unit[:, cols] = unit
        product = jnp.dot(teacher_in[...], unit, preferred_element_type=F32)
        values = jnp.exp2(product * (LOG2E / TEACHER_TEMP))
        exps[:, cols] = values
        total = jnp.sum(values, axis=0, keepdims=True)
        for tile in range(BLOCK // 128):
            col_sums[pl.ds(block * (BLOCK // 128) + tile, 1), :] = total[:, tile * 128 : (tile + 1) * 128]
        return carry

    lax.fori_loop(0, BLOCKS, teacher_block, 0)

    pl.semaphore_wait(barrier, GRP - 1 + 2 * RING - 1)

    def col_start(turn):
        message = col_sums[...].astype(BF16)
        col_send[turn] = message
        col_recv[turn, GRP - 1] = message

        for step in GRP_STEPS:
            remote(
                col_send.at[turn], col_recv.at[turn, GRP - 1 - step], col_sem.at[turn], (grp_peer(step), proto)
            ).start()

    def col_finish(turn):
        arrivals = col_recv.at[turn, pl.ds(0, GRP - 1)]
        landed(arrivals, col_sem.at[turn])
        total = col_recv[turn, 0].astype(F32)
        for slot in range(1, GRP):
            total = total + col_recv[turn, slot].astype(F32)
        col_scale[...] = 1.0 / (ALL_COLS * total)
        left(arrivals, col_sem.at[turn])

    PEERS = 2 * RING - 1

    def spread(source, slots, sem):
        slots[PEERS] = source[...]

        def send(step, base, offset):
            remote(source, slots.at[PEERS - offset - step], sem, (grp, base + z_peer(step))).start()

        def four(step, carry):
            for base, offset in ((here, 0), (across, RING)):
                send(RING // 2 - step, base, offset)
                send(RING // 2 + step, base, offset)
            return carry

        send(RING // 2, across, RING)
        send(RING // 2, here, 0)
        lax.fori_loop(1, RING // 2, four, 0)
        send(0, across, RING)

    def gathered(slots, sem):
        arrivals = slots.at[pl.ds(0, PEERS)]
        landed(arrivals, sem)
        total = None
        for index in range(RING):
            slot = lax.rem(index + RING - 1 - z + RING, RING)
            pair = slots[RING + slot] + slots[slot]
            total = pair if total is None else total + pair
        left(arrivals, sem)
        return total

    def row_start(turn, sums):
        row_send[turn] = sums
        spread(row_send.at[turn], row_recv.at[turn], row_sem.at[turn])

    def row_finish(turn):
        return gathered(row_recv.at[turn], row_sem.at[turn])

    def row_pass():
        def rows_of(block, carry):
            rows = pl.ds(pl.multiple_of(block * 64, 64), 64)
            partial = jnp.zeros((64, 128), F32)
            for tile in range(TILES):
                partial = partial + exps[rows, pl.ds(tile * 128, 128)] * col_scale[pl.ds(tile, 1), :]
            row_wide[rows, :] = partial
            return carry

        lax.fori_loop(0, ROWS // 64, rows_of, 0)
        return fold_lanes(row_wide[...])

    def target_pass():
        def rows_of(block, carry):
            rows = pl.ds(pl.multiple_of(block * 64, 64), 64)
            partial = jnp.zeros((64, 128), F32)
            for tile in range(TILES):
                cols = pl.ds(tile * 128, 128)
                scaled = exps[rows, cols] * col_scale[pl.ds(tile, 1), :]
                target_half[rows, cols] = scaled.astype(BF16)
                partial = partial + scaled
            row_wide[rows, :] = partial
            return carry

        lax.fori_loop(0, ROWS // 64, rows_of, 0)

    def col_pass():
        def block_of(block, carry):
            cols = columns(block)
            partial = jnp.zeros((8, BLOCK), F32)
            for group in range(ROWS // 8):
                rows = pl.ds(group * 8, 8)
                scale = row_wide[rows, :]
                partial = partial + exps[rows, cols] * jnp.concatenate([scale] * (BLOCK // 128), axis=1)
            total = jnp.sum(partial, axis=0, keepdims=True)
            for tile in range(BLOCK // 128):
                col_sums[pl.ds(block * (BLOCK // 128) + tile, 1), :] = total[:, tile * 128 : (tile + 1) * 128]
            return carry

        lax.fori_loop(0, BLOCKS, block_of, 0)

    mine = pl.ds(pl.multiple_of(x_lo * HALF_ROWS, HALF_ROWS), HALF_ROWS)
    other = pl.ds(pl.multiple_of((1 - x_lo) * HALF_ROWS, HALF_ROWS), HALF_ROWS)

    def unit_matmul(source, rows):
        unit_part[rows, :] = jnp.dot(source[rows, :], proto_turned[...], preferred_element_type=F32)

    def own_rows(index):
        return pl.ds(pl.multiple_of(index * OWN, OWN), OWN)

    far_rows = pl.ds(0, FAR * OWN)
    near_rows = pl.ds(0, (2 * NEAR + 1) * OWN)

    def unit_x(part):
        unit_send[part] = unit_part[other, :].astype(BF16)

        def send(sem):
            def visit(step, carry):
                rows = own_rows(z_peer(step))
                remote(unit_send.at[part, rows], unit_pair.at[part, rows], sem, partner_x).start()
                return carry

            return visit

        lax.fori_loop(NEAR + 1, RING - NEAR, send(unit_x_sem.at[part, 0]), 0)
        lax.fori_loop(RING - NEAR, RING + NEAR + 1, send(unit_x_sem.at[part, 1]), 0)

    def unit_ring(part):
        def send(step):
            peer = z_peer(step)
            rows = own_rows(peer)
            total = unit_part[own_rows(here + peer), :] + unit_pair[part, rows, :].astype(F32)
            unit_share[part, rows, :] = total.astype(BF16)
            remote(
                unit_share.at[part, rows], unit_recv.at[part, step - 1], unit_z_sem.at[part], (grp, here + peer)
            ).start()

        landed(unit_pair.at[part, far_rows], unit_x_sem.at[part, 0])
        far_steps(send)
        landed(unit_pair.at[part, near_rows], unit_x_sem.at[part, 1])
        near_steps(send)
        return unit_part[own_rows(here + z), :] + unit_pair[part, own_rows(z), :].astype(F32)

    def unit_finish(part, total):
        landed(unit_recv.at[part], unit_z_sem.at[part])
        for slot in range(RING - 1):
            total = total + unit_recv[part, slot].astype(F32)
        left(unit_pair.at[part, far_rows], unit_x_sem.at[part, 0])
        left(unit_pair.at[part, near_rows], unit_x_sem.at[part, 1])
        left(unit_recv.at[part], unit_z_sem.at[part])
        return total

    col_start(0)
    loads[1].wait()
    student_unit[...] = unit_all(student_in[...])

    def student_block(block, carry):
        cols = columns(block)
        product = jnp.dot(student_unit[...], proto_unit[:, cols], preferred_element_type=F32)
        values = jnp.exp2(product * (LOG2E / STUDENT_TEMP))
        soft[:, cols] = values
        partial = values[:, :128]
        for tile in range(1, BLOCK // 128):
            partial = partial + values[:, tile * 128 : (tile + 1) * 128]
        row_wide[...] = row_wide[...] + partial
        return carry

    row_wide[...] = jnp.zeros((ROWS, 128), F32)
    lax.fori_loop(0, BLOCKS, student_block, 0)
    row_start(3, fold_lanes(row_wide[...]))
    col_finish(0)
    row_start(0, row_pass())
    student_turned[...] = student_unit[...].astype(F32).T.astype(BF16)

    def turn_block(block, carry):
        cols = columns(block)
        proto_turned[cols, :] = proto_unit[:, cols].T
        return carry

    lax.fori_loop(0, BLOCKS, turn_block, 0)
    student_total = row_finish(3)
    row_scale = 1.0 / (ALL_ROWS * row_finish(0))

    row_wide[...] = lane_broadcast(row_scale)
    col_pass()
    col_start(1)
    row_wide[...] = lane_broadcast((1.0 / STUDENT_TEMP) / student_total)

    def soft_rows(block, carry):
        rows = pl.ds(pl.multiple_of(block * 64, 64), 64)
        scale = row_wide[rows, :]
        for tile in range(TILES):
            cols = pl.ds(tile * 128, 128)
            soft_half[rows, cols] = (soft[rows, cols] * scale).astype(BF16)
        return carry

    lax.fori_loop(0, ROWS // 64, soft_rows, 0)
    unit_matmul(soft_half, pl.ds(0, ROWS))
    unit_x(0)
    col_finish(1)
    row_start(1, row_pass())
    row_scale = 1.0 / (ALL_ROWS * row_finish(1))

    row_wide[...] = lane_broadcast(row_scale)
    col_pass()
    col_start(2)
    soft_own = unit_ring(0)
    col_finish(2)
    target_pass()
    row_start(2, fold_lanes(row_wide[...]))
    unit_matmul(target_half, other)
    unit_x(1)
    unit_matmul(target_half, mine)
    target_own = unit_ring(1)
    row_wide[...] = unit_part[:, :128] * student_unit[:, :128].astype(F32) + unit_part[:, 128:] * student_unit[
        :, 128:
    ].astype(F32)
    agreement = fold_lanes(row_wide[...])
    soft_unit = unit_finish(0, soft_own)
    row_scale = 1.0 / (ALL_ROWS * row_finish(2))
    share = jnp.log(student_total) * (1.0 / (2 * RING)) - (ALL_ROWS / STUDENT_TEMP) * row_scale * agreement
    loss_send[0] = jnp.full((1, 128), jnp.sum(share) * (1.0 / ALL_ROWS), F32)
    spread(loss_send.at[0], loss_proto, loss_sem.at[0])
    row_wide[...] = lane_broadcast((ALL_ROWS / STUDENT_TEMP) * row_scale)

    def core_copy(block):
        return remote(core_send.at[block], core_recv.at[block], core_sem.at[block], partner_core)

    def term_ring(block):
        core_copy(block).wait()
        total = term_mine[block] + core_recv[block].astype(F32)
        term_mine[block] = total
        term_send[block] = total.astype(BF16)

        for step in CHIP_STEPS:
            peer = chip_peer(step)
            remote(
                term_send.at[block, peer],
                term_recv.at[block, CHIPS - 1 - step],
                term_sem.at[block],
                (peer * 2 + core, proto),
            ).start()

    def term_block(block, carry):
        cols = columns(block, TERM_BLOCK)
        scale = jnp.concatenate([row_wide[...]] * (TERM_BLOCK // 128), axis=1)
        dlogits = (soft_half[:, cols].astype(F32) - target_half[:, cols].astype(F32) * scale).astype(BF16)
        product = jnp.dot(student_turned[...], dlogits, preferred_element_type=F32)
        term[...] = product.reshape(CHIPS, 2, SHARE, TERM_BLOCK)
        core_send[block] = term[:, 1 - core].astype(BF16)
        core_copy(block).start()
        term_mine[block] = term[:, core]
        total = jnp.sum(product * proto_in[:, cols].astype(F32), axis=0, keepdims=True) * proto_scale[:, cols]
        for tile in range(TERM_BLOCK // 128):
            dots[pl.ds(block * (TERM_BLOCK // 128) + tile, 1), :] = total[:, tile * 128 : (tile + 1) * 128]

        @pl.when(block >= LAG)
        def _():
            term_ring(block - LAG)

        return carry

    lax.fori_loop(0, TERM_BLOCKS, term_block, 0)
    lax.fori_loop(TERM_BLOCKS - LAG, TERM_BLOCKS, lambda block, carry: (term_ring(block), carry)[1], 0)

    dot_send[...] = dots[...].astype(BF16)
    dot_recv[GRP - 1] = dot_send[...]

    def dot_start(step, carry):
        remote(dot_send, dot_recv.at[GRP - 1 - step], dot_sem, (grp_peer(step), proto)).start()
        return carry

    lax.fori_loop(1, GRP, dot_start, 0)

    target_unit = unit_finish(1, target_own)
    my_rows = own_rows(here + z)
    unit_grad = soft_unit - target_unit * row_wide[my_rows, 0:1]
    wide, scaling = unit_rows(student_in[my_rows, :])
    row_dots = jnp.sum(wide * unit_grad, axis=1, keepdims=True)
    student_out[my_rows, :] = ((unit_grad - wide * row_dots) * scaling).astype(BF16)

    def out_send(step, base, sem):
        rows = student_out.at[my_rows]
        remote(rows, rows, sem, (grp, base + z_peer(step))).start()

    def forward(owner):
        rows = student_out.at[own_rows(here + owner)]
        remote(rows, rows, out_sem.at[2], partner_x).start()

    far_steps(lambda step: out_send(step, here, out_sem.at[1]))
    near_steps(lambda step: out_send(step, here, out_sem.at[0]))
    forward(z)

    loss_send[1] = gathered(loss_proto, loss_sem.at[0])
    loss_all[GRP - 1] = loss_send[1]

    def loss_start(step, carry):
        remote(loss_send.at[1], loss_all.at[GRP - 1 - step], loss_sem.at[1], (grp_peer(step), proto)).start()
        return carry

    lax.fori_loop(1, GRP, loss_start, 0)

    near_out = student_out.at[pl.ds(0, 2 * NEAR * OWN)]
    far_out = student_out.at[pl.ds(0, FAR * OWN)]
    passed_out = student_out.at[pl.ds(0, RING * OWN)]
    landed(near_out, out_sem.at[0])
    near_steps(lambda step: forward(z_peer(step)))
    landed(far_out, out_sem.at[1])
    far_steps(lambda step: forward(z_peer(step)))

    dot_arrivals = dot_recv.at[pl.ds(0, GRP - 1)]
    landed(dot_arrivals, dot_sem)
    total = dot_recv[0].astype(F32)
    for slot in range(1, GRP):
        total = total + dot_recv[slot].astype(F32)
    dots[...] = total
    left(dot_arrivals, dot_sem)
    loss_arrivals = loss_all.at[pl.ds(0, GRP - 1)]
    landed(loss_arrivals, loss_sem.at[1])
    total = jnp.zeros((1, 128), F32)
    for index in range(GRP):
        total = total + loss_all[lax.rem(index + GRP - 1 - grp + GRP, GRP)]
    loss_out[...] = total
    left(loss_arrivals, loss_sem.at[1])

    def term_finish(block, carry):
        cols = columns(block, TERM_BLOCK)

        arrivals = term_recv.at[block]
        landed(arrivals, term_sem.at[block])
        total = term_mine[block, chip]
        for slot in range(CHIPS - 1):
            total = total + term_recv[block, slot].astype(F32)
        left(arrivals, term_sem.at[block])
        scaling = proto_scale[:, cols]
        wide = proto_in[pl.ds(pl.multiple_of(grp * SHARE, SHARE), SHARE), cols].astype(F32) * scaling
        dot = jnp.concatenate(
            [dots[pl.ds(block * (TERM_BLOCK // 128) + tile, 1), :] for tile in range(TERM_BLOCK // 128)], axis=1
        )
        proto_out[:, cols] = ((total - wide * dot) * scaling).astype(BF16)
        return carry

    lax.fori_loop(0, TERM_BLOCKS, term_finish, 0)

    landed(passed_out, out_sem.at[2])
    left(near_out, out_sem.at[0])
    left(far_out, out_sem.at[1])
    left(passed_out, out_sem.at[2])


def per_device(teacher_features, student_features, prototypes):
    vmem = pltpu.VMEM
    dma = pltpu.SemaphoreType.DMA
    proto_grad, student_grad, loss = pl.pallas_call(
        kernel,
        out_shape=(
            vmem((SHARE, COLS), BF16),
            vmem((ROWS, WIDTH), BF16),
            jax.ShapeDtypeStruct((1, 128), F32),
        ),
        in_specs=[pl.BlockSpec(memory_space=pl.ANY)] * 3,
        out_specs=(pl.BlockSpec(memory_space=vmem),) * 3,
        scratch_shapes=[
            vmem((ROWS, WIDTH), BF16),
            vmem((ROWS, WIDTH), BF16),
            vmem((WIDTH, COLS), BF16),
            vmem((ROWS, WIDTH), BF16),
            vmem((WIDTH, ROWS), BF16),
            vmem((WIDTH, COLS), BF16),
            vmem((COLS, WIDTH), BF16),
            vmem((1, COLS), F32),
            vmem((ROWS, COLS), F32),
            vmem((ROWS, COLS), F32),
            vmem((ROWS, COLS), BF16),
            vmem((ROWS, COLS), BF16),
            vmem((ROWS, 128), F32),
            vmem((TILES, 128), F32),
            vmem((ITERS, TILES, 128), BF16),
            vmem((ITERS, GRP, TILES, 128), BF16),
            vmem((TILES, 128), F32),
            vmem((ITERS + 1, 4, 128), F32),
            vmem((ITERS + 1, 2 * RING, 4, 128), F32),
            vmem((2, 1, 128), F32),
            vmem((2 * RING, 1, 128), F32),
            vmem((GRP, 1, 128), F32),
            vmem((ROWS, WIDTH), F32),
            vmem((2, HALF_ROWS, WIDTH), BF16),
            vmem((2, HALF_ROWS, WIDTH), BF16),
            vmem((2, HALF_ROWS, WIDTH), BF16),
            vmem((2, RING - 1, OWN, WIDTH), BF16),
            vmem((CHIPS, 2, SHARE, TERM_BLOCK), F32),
            vmem((TERM_BLOCKS, CHIPS, SHARE, TERM_BLOCK), BF16),
            vmem((TERM_BLOCKS, CHIPS, SHARE, TERM_BLOCK), BF16),
            vmem((TERM_BLOCKS, CHIPS, SHARE, TERM_BLOCK), F32),
            vmem((TERM_BLOCKS, CHIPS, SHARE, TERM_BLOCK), BF16),
            vmem((TERM_BLOCKS, CHIPS - 1, SHARE, TERM_BLOCK), BF16),
            vmem((TILES, 128), F32),
            vmem((TILES, 128), BF16),
            vmem((GRP, TILES, 128), BF16),
            dma((2 + BLOCKS,)),
            dma((ITERS, 2)),
            dma((ITERS + 1, 2)),
            dma((2, 2)),
            dma((2, 2, 2)),
            dma((2, 2)),
            dma((3, 2)),
            dma((TERM_BLOCKS, 2)),
            dma((TERM_BLOCKS, 2)),
            dma((2,)),
        ],
        compiler_params=pltpu.CompilerParams(
            collective_id=0, has_side_effects=True, vmem_limit_bytes=56 * 2**20
        ),
        name="sinkhorn_step",
    )(teacher_features, student_features, prototypes)
    return proto_grad, student_grad, loss[0, 0]


def solution(mesh):
    placed = (P("grp", None), P("grp", None), P(None, "proto"))
    return jax.shard_map(
        per_device,
        mesh=mesh,
        in_specs=placed,
        out_specs=(P("grp", "proto"), P("grp", None), P()),
        check_vma=False,
    )
```
